32 devices in a mesh: ens: 4 (over y, x), lat: 8 (over z, core).
Axes of the slice: x: 2, y: 2, z: 4, core: 2. Of those that a mesh axis runs over, the one named last changes fastest.
Arguments:
- features: bfloat16 [32, 128, 128], P('lat'), may hold values from -6 to 6
- random_perturbation: bfloat16 [4, 32, 128, 128], P('ens', 'lat'), may hold values from -6 to 6
- observed_truth: float32 [69, 32, 128], P(None, 'lat'), may hold values from -6 to 6
- stencil_taps: float32 [49, 128], replicated, may hold values from -0.875 to 0.875
- affine_factor: float32 [128], replicated, may hold values from 0.5 to 1.5
- widen_matrix: bfloat16 [512, 128], P('lat'), may hold values from -0.5 to 0.5
- shrink_matrix: bfloat16 [512, 128], P('lat'), may hold values from -0.25 to 0.25
- readout_matrix: bfloat16 [69, 128], replicated, may hold values from -0.5 to 0.5
Outputs:
- crps_score: float32 [], replicated
- stencil_taps_sensitivity: float32 [49, 128], replicated
- affine_factor_sensitivity: float32 [128], replicated
- widen_matrix_sensitivity: float32 [512, 128], P('lat')
- shrink_matrix_sensitivity: float32 [512, 128], P('lat')
- readout_matrix_sensitivity: float32 [69, 128], replicated
- sample_outlook: bfloat16 [4, 69, 32, 128], P('ens', None, 'lat')
- sample_average_spread: float32 [4, 69, 32, 128], P('ens', None, 'lat')
The draws below stay inside these ranges and needn't reach their ends.
All inputs are finite; a program needn't handle non-finite values.
Results may differ from the reference program's by a relative error of at most 0.0024.
The reference program's roundings to bfloat16 on the way count: a program that leaves them out, or rounds other values in their place, can miss the bound.
Values may be sent and summed in bfloat16 or wider, within the bound.
A program may use at most 64 MiB of HBM per device.

```python
import math
import jax
import jax.numpy as jnp
from jax import lax

CHANNEL_COUNT = 128
EXPANSION_WIDTH = 512
OUTPUT_QUANTITY = 69
STENCIL_SIDE = 7
ZONAL_SPAN = 128
MEMBERS = 4
MERIDIAN_SPAN = 32


def block_scale(rng, dims, split, least, high):
    def one(dim, shards_of):
        draws = jax.random.uniform(jax.random.fold_in(jax.random.fold_in(rng, 6), dim), (shards_of,), jnp.float32, least / len(split), high / len(split))
        return jnp.repeat(jnp.exp(draws), dims[dim] // shards_of).reshape((-1,) + (1,) * (len(dims) - dim - 1))

    gain = one(*split[0])
    for cut in split[1:]:
        gain = gain * one(*cut)
    return gain


def gaussian(own_key, extent, scale, reach, split=(), dtype=jnp.bfloat16):
    values = scale * jax.random.normal(own_key, extent, jnp.float32)
    if split:
        values = values * block_scale(own_key, extent, split, -0.22, 0.18)
    return jnp.clip(values, -reach, reach).astype(dtype)


def setup_inputs(seed: int = 0) -> dict:
    arg_keys = jax.random.split(jax.random.key(seed), 9)
    return {
        "features": gaussian(arg_keys[0], (MERIDIAN_SPAN, ZONAL_SPAN, CHANNEL_COUNT), 1.0, 6.0, ((0, 8),)),
        "random_perturbation": gaussian(arg_keys[1], (MEMBERS, MERIDIAN_SPAN, ZONAL_SPAN, CHANNEL_COUNT), 1.0, 6.0, ((0, 4), (1, 8))),
        "observed_truth": gaussian(arg_keys[2], (OUTPUT_QUANTITY, MERIDIAN_SPAN, ZONAL_SPAN), 1.0, 6.0, ((1, 8),), jnp.float32),
        "stencil_taps": gaussian(arg_keys[3], (STENCIL_SIDE * STENCIL_SIDE, CHANNEL_COUNT), (STENCIL_SIDE * STENCIL_SIDE) ** -0.5, 0.875, (), jnp.float32),
        "affine_factor": jnp.clip(1.0 + 0.1 * jax.random.normal(arg_keys[4], (CHANNEL_COUNT,), jnp.float32), 0.5, 1.5),
        "widen_matrix": gaussian(arg_keys[5], (EXPANSION_WIDTH, CHANNEL_COUNT), CHANNEL_COUNT ** -0.5, 0.5, ((0, 8),)),
        "shrink_matrix": gaussian(arg_keys[6], (EXPANSION_WIDTH, CHANNEL_COUNT), EXPANSION_WIDTH ** -0.5, 0.25, ((0, 8),)),
        "readout_matrix": gaussian(arg_keys[7], (OUTPUT_QUANTITY, CHANNEL_COUNT), CHANNEL_COUNT ** -0.5, 0.5),
    }


SQRT_TWO_PI = 0.7978845608028654
CUBIC = 0.044715
EPSILON = 1e-06
SMOOTHING = 0.01

def smooth_magnitude(value):
    return jnp.sqrt(value * value + SMOOTHING)

def smooth_slope(value):
    return value * lax.rsqrt(value * value + SMOOTHING)

def gelu_tanh(northern_margin):
    return 0.5 * northern_margin * (1.0 + jnp.tanh(SQRT_TWO_PI * (northern_margin + CUBIC * northern_margin * northern_margin * northern_margin)))

def gelu_slope(northern_margin):
    inner = jnp.tanh(SQRT_TWO_PI * (northern_margin + CUBIC * northern_margin * northern_margin * northern_margin))
    return 0.5 * (1.0 + inner) + 0.5 * northern_margin * (1.0 - inner * inner) * SQRT_TWO_PI * (1.0 + 3.0 * CUBIC * northern_margin * northern_margin)

def depthwise(margin_extended, stencil_taps, meridian_slab):
    half = STENCIL_SIDE // 2
    wide = margin_extended.astype(jnp.float32)
    axis_rows = wide.ndim - 3
    result = jnp.zeros(wide.shape[:axis_rows] + (meridian_slab,) + wide.shape[axis_rows + 1:], jnp.float32)
    for offset_row in range(STENCIL_SIDE):
        band = lax.slice_in_dim(wide, offset_row, offset_row + meridian_slab, axis=axis_rows)
        for offset_col in range(STENCIL_SIDE):
            result = result + stencil_taps[offset_row * STENCIL_SIDE + offset_col] * jnp.roll(band, half - offset_col, axis=-2)
    return result

def kernel_grad(margin_extended, upstream, meridian_slab):
    half = STENCIL_SIDE // 2
    wide = margin_extended.astype(jnp.float32)
    axis_rows = wide.ndim - 3
    channels = upstream.shape[-1]
    taps = []
    for offset_row in range(STENCIL_SIDE):
        band = lax.slice_in_dim(wide, offset_row, offset_row + meridian_slab, axis=axis_rows)
        for offset_col in range(STENCIL_SIDE):
            shifted = jnp.roll(band, half - offset_col, axis=-2)
            taps.append(lax.optimization_barrier(jnp.sum((upstream * shifted).reshape(-1, channels), axis=0)))
    return jnp.stack(taps)

def normalize(depth_out):
    centre = lax.optimization_barrier(jnp.mean(depth_out, axis=-1, keepdims=True))
    centred = depth_out - centre
    variance = lax.optimization_barrier(jnp.mean(centred * centred, axis=-1, keepdims=True))
    reciprocal_spread = lax.rsqrt(variance + EPSILON)
    return (centred * reciprocal_spread, reciprocal_spread)

def sample_evaluation(planar_map, margin_extended, stencil_taps, affine_factor, widen_matrix, shrink_matrix, readout_matrix):
    meridian_slab, zonal_points, channels = planar_map.shape
    depth_out = depthwise(margin_extended, stencil_taps, meridian_slab)
    factor_multiplied, reciprocal_spread = normalize(depth_out)
    standardized_activation = (affine_factor * factor_multiplied).astype(jnp.bfloat16).reshape(meridian_slab * zonal_points, channels)
    northern_margin = lax.dot_general(standardized_activation, widen_matrix, (((1,), (1,)), ((), ())), preferred_element_type=jnp.float32)
    nonlinear_response = gelu_tanh(northern_margin).astype(jnp.bfloat16)
    mixed = jnp.dot(nonlinear_response, shrink_matrix, preferred_element_type=jnp.float32)
    skip_activation = (planar_map.reshape(meridian_slab * zonal_points, channels).astype(jnp.float32) + mixed).astype(jnp.bfloat16)
    sample_outlook = lax.dot_general(readout_matrix, skip_activation, (((1,), (1,)), ((), ())), preferred_element_type=jnp.float32).astype(jnp.bfloat16)
    return (sample_outlook, (factor_multiplied, reciprocal_spread, standardized_activation, northern_margin, nonlinear_response, skip_activation))

def reverse_sample_sweep(margin_extended, carried_signal, stored_intermediates, affine_factor, widen_matrix, shrink_matrix, readout_matrix):
    factor_multiplied, reciprocal_spread, standardized_activation, northern_margin, nonlinear_response, skip_activation = stored_intermediates
    meridian_slab, zonal_points, channels = factor_multiplied.shape
    readout_matrix_sensitivity = jnp.dot(carried_signal, skip_activation, preferred_element_type=jnp.float32)
    back_residual = lax.dot_general(carried_signal, readout_matrix, (((0,), (0,)), ((), ())), preferred_element_type=jnp.float32).astype(jnp.bfloat16)
    shrink_matrix_sensitivity = lax.dot_general(nonlinear_response, back_residual, (((0,), (0,)), ((), ())), preferred_element_type=jnp.float32)
    back_gate = lax.dot_general(back_residual, shrink_matrix, (((1,), (1,)), ((), ())), preferred_element_type=jnp.float32)
    back_upper = (back_gate * gelu_slope(northern_margin)).astype(jnp.bfloat16)
    widen_matrix_sensitivity = lax.dot_general(back_upper, standardized_activation, (((0,), (0,)), ((), ())), preferred_element_type=jnp.float32)
    back_norm = jnp.dot(back_upper, widen_matrix, preferred_element_type=jnp.float32).reshape(meridian_slab, zonal_points, channels)
    affine_factor_sensitivity = lax.optimization_barrier(jnp.sum((back_norm * factor_multiplied).reshape(-1, channels), axis=0))
    back_scaled = back_norm * affine_factor
    back_depth = reciprocal_spread * (back_scaled - lax.optimization_barrier(jnp.mean(back_scaled, axis=-1, keepdims=True)) - factor_multiplied * lax.optimization_barrier(jnp.mean(back_scaled * factor_multiplied, axis=-1, keepdims=True)))
    stencil_taps_sensitivity = kernel_grad(margin_extended, back_depth, meridian_slab)
    return (stencil_taps_sensitivity, affine_factor_sensitivity, widen_matrix_sensitivity, shrink_matrix_sensitivity, readout_matrix_sensitivity)

def reference(features, random_perturbation, observed_truth, stencil_taps, affine_factor, widen_matrix, shrink_matrix, readout_matrix):
    half = STENCIL_SIDE // 2
    row_index = jnp.arange(MERIDIAN_SPAN).astype(jnp.float32)
    area = jnp.cos(math.pi * ((row_index + 0.5) / MERIDIAN_SPAN - 0.5)).astype(jnp.float32)
    weight = (area * (1.0 / (MERIDIAN_SPAN * ZONAL_SPAN)))[None, None, :, None]

    def member_field(member_noise):
        planar_map = (features.astype(jnp.float32) + member_noise.astype(jnp.float32)).astype(jnp.bfloat16)
        margin_extended = jnp.pad(planar_map, ((half, half), (0, 0), (0, 0)))
        return (planar_map, margin_extended)

    def estimated_outputs(member_noise):
        planar_map, margin_extended = member_field(member_noise)
        sample_outlook, ignored_entry = sample_evaluation(planar_map, margin_extended, stencil_taps, affine_factor, widen_matrix, shrink_matrix, readout_matrix)
        return sample_outlook.reshape(OUTPUT_QUANTITY, MERIDIAN_SPAN, ZONAL_SPAN)
    sample_outlooks = lax.map(estimated_outputs, random_perturbation)
    numeric_tensor = sample_outlooks.astype(jnp.float32)

    def pair_step(carry, other):
        gap = numeric_tensor - other[None]
        return ((carry[0] + smooth_magnitude(gap), carry[1] + smooth_slope(gap)), None)
    nil_filled = jnp.zeros_like(numeric_tensor)
    (spread, ranks), ignored_entry = lax.scan(pair_step, (nil_filled, nil_filled), numeric_tensor)
    miss = numeric_tensor - observed_truth[None]
    pair_norm = 1.0 / (MEMBERS * (MEMBERS - 1))
    crps_score = jnp.sum(weight * (smooth_magnitude(miss) / MEMBERS - 0.5 * pair_norm * spread))
    flows = (weight * (smooth_slope(miss) / MEMBERS - pair_norm * ranks)).astype(jnp.bfloat16)

    def accumulate(carry, inputs):
        member_noise, sample_signal = inputs
        planar_map, margin_extended = member_field(member_noise)
        ignored_entry, stored_intermediates = sample_evaluation(planar_map, margin_extended, stencil_taps, affine_factor, widen_matrix, shrink_matrix, readout_matrix)
        sensitivities = reverse_sample_sweep(margin_extended, sample_signal.reshape(OUTPUT_QUANTITY, MERIDIAN_SPAN * ZONAL_SPAN), stored_intermediates, affine_factor, widen_matrix, shrink_matrix, readout_matrix)
        return (jax.tree.map(jnp.add, carry, sensitivities), None)
    begin_offset = (jnp.zeros((STENCIL_SIDE * STENCIL_SIDE, CHANNEL_COUNT), jnp.float32), jnp.zeros((CHANNEL_COUNT,), jnp.float32), jnp.zeros((EXPANSION_WIDTH, CHANNEL_COUNT), jnp.float32), jnp.zeros((EXPANSION_WIDTH, CHANNEL_COUNT), jnp.float32), jnp.zeros((OUTPUT_QUANTITY, CHANNEL_COUNT), jnp.float32))
    (stencil_taps_sensitivity, affine_factor_sensitivity, widen_matrix_sensitivity, shrink_matrix_sensitivity, readout_matrix_sensitivity), ignored_entry = lax.scan(accumulate, begin_offset, (random_perturbation, flows))
    sample_average_spread = spread / (MEMBERS - 1)
    return (crps_score, stencil_taps_sensitivity, affine_factor_sensitivity, widen_matrix_sensitivity, shrink_matrix_sensitivity, readout_matrix_sensitivity, sample_outlooks, sample_average_spread)
```

```python
import functools
import math

import jax
import jax.numpy as jnp
from jax import lax
from jax.experimental import pallas as pl
from jax.experimental.pallas import tpu as pltpu
from jax.sharding import PartitionSpec as P

SIDE = 7
HALF = SIDE // 2
SQRT_TWO_PI = 0.7978845608028654
CUBIC = 0.044715
EPSILON = 1e-06
SMOOTHING = 0.01
PAD = 8
GRAD_ROW = 72
SMALL_ROWS = 128
F32 = jnp.float32
BF16 = jnp.bfloat16


def dot(a, b, dims):
    return lax.dot_general(a, b, (dims, ((), ())), preferred_element_type=F32)


def kernel(
    sizes,
    feat, noise, obs, taps, gain, widen, shrink, readout,
    crps_o, taps_o, gain_o, up_o, down_o, out_o, look_o, spread_o,
    ext, wide, tapb, depth, scaled_s, inv_s, normed, upper, inner, gated, ro, looks, wbuf,
    grads, rec_a, part_b, rec_b, part_c, rec_c, rec_d,
    small, small_a, small_pb, small_b, small_pc, small_c, small_d,
    halo_send, halo_recv, w_send, w_fwd, w_recv, e_send, e_recv,
    a_send, a_recv, b_send, b_recv, c_send, c_recv, d_send, d_recv,
):
    E, L = sizes
    Z = L // 2
    slab, zonal, channels = feat.shape
    quantities = obs.shape[0]
    rows = ro.shape[0]
    points = slab * zonal
    hidden = L * widen.shape[0]
    piece = widen.shape[0] // E
    ens = lax.axis_index("ens")
    lat = lax.axis_index("lat")
    z = lat // 2
    core = lat % 2
    sibling = z * 2 + (1 - core)

    def at(e, l):
        return {"ens": e, "lat": l}

    def remote(src, dst, send, recv, where):
        return pltpu.make_async_remote_copy(
            src_ref=src, dst_ref=dst, send_sem=send, recv_sem=recv,
            device_id=where, device_id_type=pl.DeviceIdType.MESH,
        )

    barrier = pltpu.get_barrier_semaphore()
    for k in range(1, L):
        pl.semaphore_signal(barrier, inc=1, device_id=at(ens, (lat + k) % L),
                            device_id_type=pl.DeviceIdType.MESH)
    for k in range(1, E):
        pl.semaphore_signal(barrier, inc=1, device_id=at((ens + k) % E, lat),
                            device_id_type=pl.DeviceIdType.MESH)

    def widen_rows(start, count):
        block = ext[start : start + count].astype(F32)
        wide[start : start + count, PAD : PAD + zonal, :] = block
        wide[start : start + count, 0:PAD, :] = block[:, zonal - PAD :, :]
        wide[start : start + count, PAD + zonal :, :] = block[:, :PAD, :]

    field = (feat[...].astype(F32) + noise[0].astype(F32)).astype(BF16)
    ext[HALF : HALF + slab] = field
    wbuf[pl.ds(lat, 1), 0] = widen[...][None]
    wbuf[pl.ds(lat, 1), 1] = shrink[...][None]
    pl.semaphore_wait(barrier, L - 1 + E - 1)

    south = remote(ext.at[pl.ds(slab, HALF)], ext.at[pl.ds(0, HALF)],
                   halo_send.at[0], halo_recv.at[0], at(ens, jnp.minimum(lat + 1, L - 1)))
    north = remote(ext.at[pl.ds(HALF, HALF)], ext.at[pl.ds(HALF + slab, HALF)],
                   halo_send.at[1], halo_recv.at[1], at(ens, jnp.maximum(lat - 1, 0)))

    @pl.when(lat < L - 1)
    def _():
        south.start()

    @pl.when(lat > 0)
    def _():
        north.start()

    own = [
        remote(wbuf.at[lat], wbuf.at[lat], w_send.at[k], w_recv.at[lat],
               at(ens, ((z + k) % Z) * 2 + core))
        for k in range(1, Z)
    ]
    for copy in own:
        copy.start()
    forwards = [remote(wbuf.at[lat], wbuf.at[lat], w_fwd.at[0], w_recv.at[lat], at(ens, sibling))]
    forwards[0].start()

    widen_rows(HALF, slab)
    for t in range(SIDE * SIDE):
        tapb[t] = jnp.broadcast_to(taps[t : t + 1, :], (8, channels))
    ro[...] = jnp.zeros_like(ro)
    ro[0:quantities, :] = readout[...]

    step = 32

    def convolve(ext_rows, fresh):
        def body(t, carry):
            base = pl.multiple_of(t * step, step)
            sums = []
            for i in range(slab):
                if fresh:
                    sums.append(jnp.zeros((step // 8, 8, channels), F32))
                else:
                    sums.append(depth[i, pl.ds(base, step), :].reshape(step // 8, 8, channels))
            for b in range(SIDE):
                for r in ext_rows:
                    x = wide[r, pl.ds(base + PAD - HALF + b, step), :].reshape(
                        step // 8, 8, channels)
                    for i in range(slab):
                        a = r - i
                        if 0 <= a < SIDE:
                            sums[i] = sums[i] + tapb[a * SIDE + b] * x
            for i in range(slab):
                depth[i, pl.ds(base, step), :] = sums[i].reshape(step, channels)
            return carry

        lax.fori_loop(0, zonal // step, body, 0)

    convolve(range(HALF, HALF + slab), True)

    for k in range(1, Z):
        other = ((z + k) % Z) * 2 + core
        remote(wbuf.at[other], wbuf.at[other], w_send.at[k], w_recv.at[other],
               at(ens, other)).wait_recv()
        copy = remote(wbuf.at[other], wbuf.at[other], w_fwd.at[k], w_recv.at[other],
                      at(ens, sibling))
        copy.start()
        forwards.append(copy)

    @pl.when(lat > 0)
    def _():
        south.wait_recv()
        widen_rows(0, HALF)

    @pl.when(lat == 0)
    def _():
        wide[0:HALF] = jnp.zeros((HALF, zonal + 2 * PAD, channels), F32)

    @pl.when(lat < L - 1)
    def _():
        north.wait_recv()
        widen_rows(HALF + slab, HALF)

    @pl.when(lat == L - 1)
    def _():
        wide[HALF + slab :] = jnp.zeros((HALF, zonal + 2 * PAD, channels), F32)

    convolve([*range(HALF), *range(HALF + slab, 2 * HALF + slab)], False)

    for i in range(slab):
        d = depth[i]
        centred = d - jnp.mean(d, axis=-1, keepdims=True)
        inverse = lax.rsqrt(jnp.mean(centred * centred, axis=-1, keepdims=True) + EPSILON)
        scaled = centred * inverse
        scaled_s[i] = scaled
        inv_s[i] = jnp.broadcast_to(inverse, (zonal, channels))
        normed[i * zonal : (i + 1) * zonal, :] = (gain[...] * scaled).astype(BF16)

    for k in range(Z):
        other = ((z + k) % Z) * 2 + (1 - core)
        remote(wbuf.at[other], wbuf.at[other], w_fwd.at[k], w_recv.at[other],
               at(ens, sibling)).wait_recv()

    up = wbuf[:, 0].reshape(hidden, channels)
    down = wbuf[:, 1].reshape(hidden, channels)
    upper[...] = dot(normed[...], up, ((1,), (1,)))

    sub = 16

    def gelu_step(t, carry):
        span = pl.ds(pl.multiple_of(t * sub, sub), sub)
        u = upper[span, :]
        th = jnp.tanh(SQRT_TWO_PI * (u + CUBIC * u * u * u))
        inner[span, :] = th
        gated[span, :] = (0.5 * u * (1.0 + th)).astype(BF16)
        return carry

    lax.fori_loop(0, points // sub, gelu_step, 0)

    mixed = dot(gated[...], down, ((1,), (0,)))
    residual = (
        ext[HALF : HALF + slab].reshape(points, channels).astype(F32) + mixed
    ).astype(BF16)
    mine = dot(ro[...], residual, ((1,), (1,))).astype(BF16)
    looks[pl.ds(ens, 1)] = mine[None]

    shares = [
        remote(looks.at[ens], looks.at[ens], e_send.at[k], e_recv.at[ens], at((ens + k) % E, lat))
        for k in range(1, E)
    ]
    for copy in shares:
        copy.start()

    look_o[...] = mine[:quantities]
    mine = mine.astype(F32)

    def slope_step(t, carry):
        span = pl.ds(pl.multiple_of(t * sub, sub), sub)
        u = upper[span, :]
        th = inner[span, :]
        inner[span, :] = 0.5 * (1.0 + th) + 0.5 * u * (1.0 - th * th) * SQRT_TWO_PI * (
            1.0 + 3.0 * CUBIC * u * u
        )
        return carry

    lax.fori_loop(0, points // sub, slope_step, 0)

    members = E
    pair_norm = 1.0 / (members * (members - 1))
    latitudes = slab * L
    cell = lax.broadcasted_iota(jnp.int32, (8, points), 1) // zonal + lat * slab
    area = jnp.cos(math.pi * ((cell.astype(F32) + 0.5) / latitudes - 0.5))
    weight = (area * (1.0 / (latitudes * zonal)))[0:1]

    truth = jnp.concatenate([obs[:, i, :] for i in range(slab)], axis=1)
    truth = jnp.concatenate([truth, jnp.zeros((rows - quantities, points), F32)], axis=0)
    miss = mine - truth
    square = miss * miss + SMOOTHING
    root = lax.rsqrt(square)
    miss_size = square * root
    miss_slope = miss * root

    spread = jnp.full((rows, points), math.sqrt(SMOOTHING), F32)
    ranks = jnp.zeros((rows, points), F32)
    for k in range(1, E):
        other = (ens + k) % E
        remote(looks.at[other], looks.at[other], e_send.at[k], e_recv.at[other],
               at(other, lat)).wait_recv()
        gap = mine - looks[pl.ds(other, 1)][0].astype(F32)
        square = gap * gap + SMOOTHING
        root = lax.rsqrt(square)
        spread = spread + square * root
        ranks = ranks + gap * root
    spread_o[...] = spread[:quantities] * (1.0 / (members - 1))
    loss = weight * (miss_size / members - 0.5 * pair_norm * spread)
    loss = jnp.sum(jnp.sum(loss[:quantities], axis=0, keepdims=True), axis=1, keepdims=True)
    flow = (weight * (miss_slope / members - pair_norm * ranks)).astype(BF16)

    def stash(slot, value):
        for l in range(L):
            for e in range(E):
                begin = (l * E + e) * piece
                grads[slot, l % 2, e, l // 2] = value[begin : begin + piece]

    def start_a(slot):
        copy = remote(grads.at[slot, 1 - core], rec_a.at[slot], a_send.at[slot], a_recv.at[slot],
                      at(ens, sibling))
        copy.start()
        return [copy]

    def scatter(src, dst, send, recv, me, count, place):
        copies = [
            remote(src((me + k) % count), dst.at[me], send.at[k], recv.at[me],
                   place((me + k) % count))
            for k in range(1, count)
        ]
        for copy in copies:
            copy.start()
        return copies

    def arrive(dst, send, recv, me, count, place):
        for k in range(1, count):
            other = (me + k) % count
            remote(dst.at[other], dst.at[other], send.at[k], recv.at[other],
                   place(other)).wait_recv()

    def by_ens(e):
        return at(e, lat)

    def by_z(other):
        return at(ens, other * 2 + core)

    def start_b(slot):
        sent = remote(grads.at[slot, 1 - core], rec_a.at[slot], a_send.at[slot], a_recv.at[slot],
                      at(ens, sibling))
        sent.wait_recv()
        part_b[slot] = grads[slot, pl.ds(core, 1)][0] + rec_a[slot]
        rec_b[slot, pl.ds(ens, 1)] = part_b[slot, pl.ds(ens, 1)]
        return scatter(lambda e: part_b.at[slot, e], rec_b.at[slot], b_send.at[slot],
                       b_recv.at[slot], ens, E, by_ens)

    def start_c(slot):
        arrive(rec_b.at[slot], b_send.at[slot], b_recv.at[slot], ens, E, by_ens)
        total = rec_b[slot, 0]
        for e in range(1, E):
            total = total + rec_b[slot, e]
        part_c[slot] = total
        rec_c[slot, pl.ds(z, 1)] = part_c[slot, pl.ds(z, 1)]
        return scatter(lambda o: part_c.at[slot, o], rec_c.at[slot], c_send.at[slot],
                       c_recv.at[slot], z, Z, by_z)

    def start_d(slot):
        arrive(rec_c.at[slot], c_send.at[slot], c_recv.at[slot], z, Z, by_z)
        total = rec_c[slot, 0]
        for o in range(1, Z):
            total = total + rec_c[slot, o]
        rec_d[slot, pl.ds(ens, 1)] = total[None]
        return scatter(lambda e: rec_d.at[slot, ens], rec_d.at[slot], d_send.at[slot],
                       d_recv.at[slot], ens, E, by_ens)

    def finish(slot, out):
        arrive(rec_d.at[slot], d_send.at[slot], d_recv.at[slot], ens, E, by_ens)
        for e in range(E):
            out[e * piece : (e + 1) * piece, :] = rec_d[slot, e]

    sent = []
    back_residual = dot(flow, ro[...], ((0,), (0,))).astype(BF16)
    stash(0, dot(gated[...], back_residual, ((0,), (0,))))
    sent += start_a(0)

    upper[...] = dot(back_residual, down, ((1,), (1,)))

    def back_step(t, carry):
        span = pl.ds(pl.multiple_of(t * sub, sub), sub)
        gated[span, :] = (upper[span, :] * inner[span, :]).astype(BF16)
        return carry

    lax.fori_loop(0, points // sub, back_step, 0)
    stash(1, dot(gated[...], normed[...], ((0,), (0,))))
    sent += start_a(1)
    sent += start_b(0)

    out_grad = dot(flow, residual, ((1,), (0,)))
    chunk = SMALL_ROWS // E

    def put(row, value):
        done = 0
        count = value.shape[0]
        while done < count:
            block, offset = divmod(row + done, chunk)
            take = min(count - done, chunk - offset)
            small[block, offset : offset + take, :] = value[done : done + take]
            done += take

    put(0, out_grad[:GRAD_ROW])

    upper[:, 0:channels] = dot(gated[...], up, ((1,), (0,)))
    gain_sum = jnp.zeros((1, channels), F32)
    for i in range(slab):
        back_norm = upper[i * zonal : (i + 1) * zonal, 0:channels]
        scaled = scaled_s[i]
        gain_sum = gain_sum + jnp.sum(back_norm * scaled, axis=0, keepdims=True)
        g = back_norm * gain[...]
        depth[i] = inv_s[i] * (
            g
            - jnp.mean(g, axis=-1, keepdims=True)
            - scaled * jnp.mean(g * scaled, axis=-1, keepdims=True)
        )
    sent += start_b(1)

    lane = 16
    for b in range(SIDE):
        def body(t, sums):
            base = pl.multiple_of(t * lane, lane)
            sums = list(sums)
            g = [depth[i, pl.ds(base, lane), :] for i in range(slab)]
            for r in range(2 * HALF + slab):
                x = wide[r, pl.ds(base + PAD - HALF + b, lane), :]
                for i in range(slab):
                    a = r - i
                    if 0 <= a < SIDE:
                        sums[a] = sums[a] + g[i] * x
            return tuple(sums)

        sums = lax.fori_loop(
            0, zonal // lane, body, tuple(jnp.zeros((lane, channels), F32) for _ in range(SIDE))
        )
        for a in range(SIDE):
            put(GRAD_ROW + a * SIDE + b, jnp.sum(sums[a], axis=0, keepdims=True))
    tail = GRAD_ROW + SIDE * SIDE
    put(tail, gain_sum)
    put(tail + 1, jnp.broadcast_to(loss, (1, channels)))
    put(tail + 2, jnp.zeros((SMALL_ROWS - tail - 2, channels), F32))

    copy = remote(small, small_a, a_send.at[2], a_recv.at[2], at(ens, sibling))
    copy.start()
    sent.append(copy)
    sent += start_c(0)
    copy.wait_recv()
    small_pb[...] = small[...] + small_a[...]
    small_b[pl.ds(ens, 1)] = small_pb[pl.ds(ens, 1)]
    sent += scatter(lambda e: small_pb.at[e], small_b, b_send.at[2], b_recv.at[2], ens, E, by_ens)
    sent += start_c(1)
    sent += start_d(0)
    arrive(small_b, b_send.at[2], b_recv.at[2], ens, E, by_ens)
    total = small_b[0]
    for e in range(1, E):
        total = total + small_b[e]
    small_pc[...] = total
    small_c[pl.ds(z, 1)] = total[None]
    sent += scatter(lambda o: small_pc, small_c, c_send.at[2], c_recv.at[2], z, Z, by_z)
    sent += start_d(1)
    arrive(small_c, c_send.at[2], c_recv.at[2], z, Z, by_z)
    total = small_c[0]
    for o in range(1, Z):
        total = total + small_c[o]
    small_d[pl.ds(ens, 1)] = total[None]
    sent += scatter(lambda e: small_d.at[ens], small_d, d_send.at[2], d_recv.at[2], ens, E, by_ens)
    finish(0, down_o)
    finish(1, up_o)
    arrive(small_d, d_send.at[2], d_recv.at[2], ens, E, by_ens)
    final = small_d[...].reshape(SMALL_ROWS, channels)
    out_o[...] = final[:quantities]
    taps_o[...] = final[GRAD_ROW:tail]
    gain_o[...] = final[tail : tail + 1]
    crps_o[...] = final[tail + 1 : tail + 2, 0:1]

    for copy in own + forwards + shares + sent:
        copy.wait_send()

    @pl.when(lat < L - 1)
    def _():
        south.wait_send()

    @pl.when(lat > 0)
    def _():
        north.wait_send()


def on_device(
    features, random_perturbation, observed_truth, stencil_taps,
    affine_factor, widen_matrix, shrink_matrix, readout_matrix,
):
    E, L = lax.axis_size("ens"), lax.axis_size("lat")
    Z = L // 2
    _, slab, zonal, channels = random_perturbation.shape
    quantities = readout_matrix.shape[0]
    unit = widen_matrix.shape[0]
    hidden = unit * L
    piece = unit // E
    points = slab * zonal
    rows = -(-quantities // 16) * 16
    chunk = SMALL_ROWS // E
    vmem = pl.BlockSpec(memory_space=pltpu.VMEM)
    dma = pltpu.SemaphoreType.DMA
    out = jax.ShapeDtypeStruct
    crps, taps, gain, up, down, head, look, spread = pl.pallas_call(
        functools.partial(kernel, (E, L)),
        out_shape=[
            out((1, 1), F32),
            out((SIDE * SIDE, channels), F32),
            out((1, channels), F32),
            out((unit, channels), F32),
            out((unit, channels), F32),
            out((quantities, channels), F32),
            out((quantities, points), BF16),
            out((quantities, points), F32),
        ],
        in_specs=[vmem] * 8,
        out_specs=[vmem] * 8,
        scratch_shapes=[
            pltpu.VMEM((slab + 2 * HALF, zonal, channels), BF16),
            pltpu.VMEM((slab + 2 * HALF, zonal + 2 * PAD, channels), F32),
            pltpu.VMEM((SIDE * SIDE, 8, channels), F32),
            pltpu.VMEM((slab, zonal, channels), F32),
            pltpu.VMEM((slab, zonal, channels), F32),
            pltpu.VMEM((slab, zonal, channels), F32),
            pltpu.VMEM((points, channels), BF16),
            pltpu.VMEM((points, hidden), F32),
            pltpu.VMEM((points, hidden), F32),
            pltpu.VMEM((points, hidden), BF16),
            pltpu.VMEM((rows, channels), BF16),
            pltpu.VMEM((E, rows, points), BF16),
            pltpu.VMEM((L, 2, unit, channels), BF16),
            pltpu.VMEM((2, 2, E, Z, piece, channels), F32),
            pltpu.VMEM((2, E, Z, piece, channels), F32),
            pltpu.VMEM((2, E, Z, piece, channels), F32),
            pltpu.VMEM((2, E, Z, piece, channels), F32),
            pltpu.VMEM((2, Z, piece, channels), F32),
            pltpu.VMEM((2, Z, piece, channels), F32),
            pltpu.VMEM((2, E, piece, channels), F32),
            pltpu.VMEM((E, chunk, channels), F32),
            pltpu.VMEM((E, chunk, channels), F32),
            pltpu.VMEM((E, chunk, channels), F32),
            pltpu.VMEM((E, chunk, channels), F32),
            pltpu.VMEM((chunk, channels), F32),
            pltpu.VMEM((Z, chunk, channels), F32),
            pltpu.VMEM((E, chunk, channels), F32),
            dma((2,)), dma((2,)),
            dma((Z,)), dma((Z,)), dma((L,)),
            dma((E,)), dma((E,)),
            dma((3,)), dma((3,)),
            dma((3, E)), dma((3, E)),
            dma((3, Z)), dma((3, Z)),
            dma((3, E)), dma((3, E)),
        ],
        compiler_params=pltpu.CompilerParams(
            collective_id=0, has_side_effects=True, vmem_limit_bytes=40 * 1024 * 1024
        ),
        cost_estimate=pl.CostEstimate(
            flops=12 * points * channels * hidden, bytes_accessed=2_000_000, transcendentals=0
        ),
    )(
        features, random_perturbation, observed_truth, stencil_taps,
        affine_factor.reshape(1, channels), widen_matrix, shrink_matrix, readout_matrix,
    )
    grid = (1, quantities, slab, zonal)
    return (
        crps.reshape(()), taps, gain.reshape(channels), up, down, head,
        look.reshape(grid), spread.reshape(grid),
    )


def solution(mesh):
    in_specs = (
        P("lat", None, None),
        P("ens", "lat", None, None),
        P(None, "lat", None),
        P(),
        P(),
        P("lat", None),
        P("lat", None),
        P(),
    )
    out_specs = (
        P(),
        P(),
        P(),
        P("lat", None),
        P("lat", None),
        P(),
        P("ens", None, "lat", None),
        P("ens", None, "lat", None),
    )
    return jax.shard_map(
        on_device, mesh=mesh, in_specs=in_specs, out_specs=out_specs, check_vma=False
    )
```

```python
import functools
import math

import jax
import jax.numpy as jnp
from jax import lax
from jax.experimental import pallas as pl
from jax.experimental.pallas import tpu as pltpu
from jax.sharding import PartitionSpec as P

SIDE = 7
HALF = SIDE // 2
SQRT_TWO_PI = 0.7978845608028654
CUBIC = 0.044715
EPSILON = 1e-06
SMOOTHING = 0.01
PAD = 8
GRAD_ROW = 72
SMALL_ROWS = 128
F32 = jnp.float32
BF16 = jnp.bfloat16


def dot(a, b, dims):
    return lax.dot_general(a, b, (dims, ((), ())), preferred_element_type=F32)


def kernel(
    sizes,
    feat_h, noise_h, obs_h, taps_h, gain_h, widen_h, shrink_h, readout_h,
    crps_o, taps_o, gain_o, up_o, down_o, out_o, look_o, spread_o,
    feat, noise, obs, taps, gain, readout,
    ext, wide, tapb, depth, scaled_s, inv_s, normed, upper, inner, gated, ro, looks, wbuf,
    resid, flows, back, gated_back, outlook, tap_grad,
    grads, rec_a, part_b, rec_b, part_c, rec_c, rec_d,
    small, small_b, small_pc, small_c, small_d,
    in_sem, halo_send, halo_recv, w_send, w_fwd, w_recv, e_send, e_recv,
    a_send, a_recv, b_send, b_recv, c_send, c_recv, d_send, d_recv,
    p_send, p_recv, q_send, q_recv, r_send, r_recv,
):
    E, L = sizes
    Z = L // 2
    slab, zonal, channels = feat.shape
    quantities = obs.shape[0]
    rows = ro.shape[0]
    points = slab * zonal
    hidden = L * wbuf.shape[2]
    piece = wbuf.shape[2] // E
    ens = lax.axis_index("ens")
    lat = lax.axis_index("lat")
    z = lat // 2
    core = lat % 2
    sibling = z * 2 + (1 - core)

    def at(e, l):
        return {"ens": e, "lat": l}

    def remote(src, dst, send, recv, where):
        return pltpu.make_async_remote_copy(
            src_ref=src, dst_ref=dst, send_sem=send, recv_sem=recv,
            device_id=where, device_id_type=pl.DeviceIdType.MESH,
        )

    barrier = pltpu.get_barrier_semaphore()
    for k in range(1, L):
        pl.semaphore_signal(barrier, inc=1, device_id=at(ens, (lat + k) % L),
                            device_id_type=pl.DeviceIdType.MESH)
    for k in range(1, E):
        for l in (lat, sibling):
            pl.semaphore_signal(barrier, inc=1, device_id=at((ens + k) % E, l),
                                device_id_type=pl.DeviceIdType.MESH)

    loads = [
        pltpu.make_async_copy(src, dst, in_sem.at[n])
        for n, (src, dst) in enumerate([
            (feat_h, feat), (noise_h, noise), (widen_h, wbuf.at[lat, 0]),
            (shrink_h, wbuf.at[lat, 1]), (taps_h, taps), (readout_h, readout),
            (gain_h, gain), (obs_h, obs),
        ])
    ]
    for copy in loads:
        copy.start()

    def widen_rows(start, count):
        block = ext[start : start + count].astype(F32)
        wide[start : start + count, PAD : PAD + zonal, :] = block
        wide[start : start + count, 0:PAD, :] = block[:, zonal - PAD :, :]
        wide[start : start + count, PAD + zonal :, :] = block[:, :PAD, :]

    loads[0].wait()
    loads[1].wait()
    field = (feat[...].astype(F32) + noise[0].astype(F32)).astype(BF16)
    ext[HALF : HALF + slab] = field
    pl.semaphore_wait(barrier, L - 1 + 2 * (E - 1))

    south = remote(ext.at[pl.ds(slab, HALF)], ext.at[pl.ds(0, HALF)],
                   halo_send.at[0], halo_recv.at[0], at(ens, jnp.minimum(lat + 1, L - 1)))
    north = remote(ext.at[pl.ds(HALF, HALF)], ext.at[pl.ds(HALF + slab, HALF)],
                   halo_send.at[1], halo_recv.at[1], at(ens, jnp.maximum(lat - 1, 0)))

    @pl.when(lat < L - 1)
    def _():
        south.start()

    @pl.when(lat > 0)
    def _():
        north.start()

    own = [
        remote(wbuf.at[lat], wbuf.at[lat], w_send.at[k], w_recv.at[lat],
               at(ens, ((z + k) % Z) * 2 + core))
        for k in range(1, Z)
    ]
    loads[2].wait()
    loads[3].wait()
    for copy in own:
        copy.start()
    forwards = [remote(wbuf.at[lat], wbuf.at[lat], w_fwd.at[0], w_recv.at[lat], at(ens, sibling))]
    forwards[0].start()

    widen_rows(HALF, slab)
    for copy in loads[4:]:
        copy.wait()
    for t in range(SIDE * SIDE):
        tapb[t] = jnp.broadcast_to(taps[t : t + 1, :], (8, channels))
    ro[...] = jnp.zeros_like(ro)
    ro[0:quantities, :] = readout[...]

    step = 32

    def convolve(ext_rows, fresh):
        def body(t, carry):
            base = pl.multiple_of(t * step, step)
            sums = []
            for i in range(slab):
                if fresh:
                    sums.append(jnp.zeros((step // 8, 8, channels), F32))
                else:
                    sums.append(depth[i, pl.ds(base, step), :].reshape(step // 8, 8, channels))
            for b in range(SIDE):
                for r in ext_rows:
                    x = wide[r, pl.ds(base + PAD - HALF + b, step), :].reshape(
                        step // 8, 8, channels)
                    for i in range(slab):
                        a = r - i
                        if 0 <= a < SIDE:
                            sums[i] = sums[i] + tapb[a * SIDE + b] * x
            for i in range(slab):
                depth[i, pl.ds(base, step), :] = sums[i].reshape(step, channels)
            return carry

        lax.fori_loop(0, zonal // step, body, 0)

    convolve(range(HALF, HALF + slab), True)

    for k in range(1, Z):
        other = ((z + k) % Z) * 2 + core
        remote(wbuf.at[other], wbuf.at[other], w_send.at[k], w_recv.at[other],
               at(ens, other)).wait_recv()
        copy = remote(wbuf.at[other], wbuf.at[other], w_fwd.at[k], w_recv.at[other],
                      at(ens, sibling))
        copy.start()
        forwards.append(copy)

    @pl.when(lat > 0)
    def _():
        south.wait_recv()
        widen_rows(0, HALF)

    @pl.when(lat == 0)
    def _():
        wide[0:HALF] = jnp.zeros((HALF, zonal + 2 * PAD, channels), F32)

    @pl.when(lat < L - 1)
    def _():
        north.wait_recv()
        widen_rows(HALF + slab, HALF)

    @pl.when(lat == L - 1)
    def _():
        wide[HALF + slab :] = jnp.zeros((HALF, zonal + 2 * PAD, channels), F32)

    convolve([*range(HALF), *range(HALF + slab, 2 * HALF + slab)], False)

    for i in range(slab):
        d = depth[i]
        centred = d - jnp.mean(d, axis=-1, keepdims=True)
        inverse = lax.rsqrt(jnp.mean(centred * centred, axis=-1, keepdims=True) + EPSILON)
        scaled = centred * inverse
        scaled_s[i] = scaled
        inv_s[i] = jnp.broadcast_to(inverse, (zonal, channels))
        normed[i * zonal : (i + 1) * zonal, :] = (gain[...] * scaled).astype(BF16)

    for k in range(Z):
        other = ((z + k) % Z) * 2 + (1 - core)
        remote(wbuf.at[other], wbuf.at[other], w_fwd.at[k], w_recv.at[other],
               at(ens, sibling)).wait_recv()

    up = wbuf[:, 0].reshape(hidden, channels)
    down = wbuf[:, 1].reshape(hidden, channels)
    sub = 32
    shares = []
    for i in range(slab):
        begin, end = i * zonal, (i + 1) * zonal
        upper[begin:end, :] = dot(normed[begin:end, :], up, ((1,), (1,)))
        for t in range(begin, end, sub):
            u = upper[t : t + sub, :]
            th = jnp.tanh(SQRT_TWO_PI * (u + CUBIC * u * u * u))
            inner[t : t + sub, :] = th
            gated[t : t + sub, :] = (0.5 * u * (1.0 + th)).astype(BF16)
        mixed = dot(gated[begin:end, :], down, ((1,), (0,)))
        residual = (ext[HALF + i].astype(F32) + mixed).astype(BF16)
        resid[begin:end, :] = residual
        mine = dot(ro[...], residual, ((1,), (1,))).astype(BF16)
        looks[i, pl.ds(ens, 1)] = mine[None]
        for k in range(1, E):
            copy = remote(looks.at[i, ens], looks.at[i, ens], e_send.at[i, k], e_recv.at[i, ens],
                          at((ens + k) % E, lat))
            copy.start()
            shares.append(copy)
        outlook[:, i, :] = mine.astype(F32)

    look_o[0] = outlook[0:quantities].astype(BF16)

    for t in range(0, points, sub):
        u = upper[t : t + sub, :]
        th = inner[t : t + sub, :]
        inner[t : t + sub, :] = 0.5 * (1.0 + th) + 0.5 * u * (1.0 - th * th) * SQRT_TWO_PI * (
            1.0 + 3.0 * CUBIC * u * u
        )

    members = E
    pair_norm = 1.0 / (members * (members - 1))
    latitudes = slab * L
    loss = jnp.zeros((1, channels), F32)
    for i in range(slab):
        begin, end = i * zonal, (i + 1) * zonal
        row = jnp.full((8, zonal), lat * slab + i, jnp.int32).astype(F32)
        area = jnp.cos(math.pi * ((row + 0.5) / latitudes - 0.5))
        weight = (area * (1.0 / (latitudes * zonal)))[0:1]
        mine = looks[i, pl.ds(ens, 1)][0].astype(F32)
        truth = jnp.concatenate(
            [obs[:, i, :], jnp.zeros((rows - quantities, zonal), F32)], axis=0)
        miss = mine - truth
        square = miss * miss + SMOOTHING
        root = lax.rsqrt(square)
        miss_size = square * root
        miss_slope = miss * root
        spread = jnp.full((rows, zonal), math.sqrt(SMOOTHING), F32)
        ranks = jnp.zeros((rows, zonal), F32)
        for k in range(1, E):
            other = (ens + k) % E
            remote(looks.at[i, other], looks.at[i, other], e_send.at[i, k], e_recv.at[i, other],
                   at(other, lat)).wait_recv()
            gap = mine - looks[i, pl.ds(other, 1)][0].astype(F32)
            square = gap * gap + SMOOTHING
            root = lax.rsqrt(square)
            spread = spread + square * root
            ranks = ranks + gap * root
        spread_o[0, :, i, :] = spread[:quantities] * (1.0 / (members - 1))
        part = weight * (miss_size / members - 0.5 * pair_norm * spread)
        loss = loss + jnp.sum(part[:quantities], axis=0, keepdims=True)
        flow = (weight * (miss_slope / members - pair_norm * ranks)).astype(BF16)
        flows[:, begin:end] = flow
        back_residual = dot(flow, ro[...], ((0,), (0,))).astype(BF16)
        back[begin:end, :] = back_residual
        upper[begin:end, :] = dot(back_residual, down, ((1,), (1,)))
        for t in range(begin, end, sub):
            gated_back[t : t + sub, :] = (
                upper[t : t + sub, :] * inner[t : t + sub, :]).astype(BF16)
    loss = jnp.sum(loss, axis=1, keepdims=True)

    def stash(slot, value):
        for l in range(L):
            for e in range(E):
                begin = (l * E + e) * piece
                grads[slot, l % 2, e, l // 2] = value[begin : begin + piece]

    def start_a(slot):
        copy = remote(grads.at[slot, 1 - core], rec_a.at[slot], a_send.at[slot], a_recv.at[slot],
                      at(ens, sibling))
        copy.start()
        return [copy]

    def scatter(src, dst, send, recv, me, count, place):
        copies = [
            remote(src((me + k) % count), dst.at[me], send.at[k], recv.at[me],
                   place((me + k) % count))
            for k in range(1, count)
        ]
        for copy in copies:
            copy.start()
        return copies

    def arrive(dst, send, recv, me, count, place):
        for k in range(1, count):
            other = (me + k) % count
            remote(dst.at[other], dst.at[other], send.at[k], recv.at[other],
                   place(other)).wait_recv()

    def by_ens(e):
        return at(e, lat)

    def by_z(other):
        return at(ens, other * 2 + core)

    def start_b(slot):
        sent = remote(grads.at[slot, 1 - core], rec_a.at[slot], a_send.at[slot], a_recv.at[slot],
                      at(ens, sibling))
        sent.wait_recv()
        part_b[slot] = grads[slot, pl.ds(core, 1)][0] + rec_a[slot]
        rec_b[slot, pl.ds(ens, 1)] = part_b[slot, pl.ds(ens, 1)]
        return scatter(lambda e: part_b.at[slot, e], rec_b.at[slot], b_send.at[slot],
                       b_recv.at[slot], ens, E, by_ens)

    def start_c(slot):
        arrive(rec_b.at[slot], b_send.at[slot], b_recv.at[slot], ens, E, by_ens)
        total = rec_b[slot, 0]
        for e in range(1, E):
            total = total + rec_b[slot, e]
        part_c[slot] = total
        rec_c[slot, pl.ds(z, 1)] = part_c[slot, pl.ds(z, 1)]
        return scatter(lambda o: part_c.at[slot, o], rec_c.at[slot], c_send.at[slot],
                       c_recv.at[slot], z, Z, by_z)

    def start_d(slot):
        arrive(rec_c.at[slot], c_send.at[slot], c_recv.at[slot], z, Z, by_z)
        total = rec_c[slot, 0]
        for o in range(1, Z):
            total = total + rec_c[slot, o]
        rec_d[slot, pl.ds(ens, 1)] = total[None]
        return scatter(lambda e: rec_d.at[slot, ens], rec_d.at[slot], d_send.at[slot],
                       d_recv.at[slot], ens, E, by_ens)

    def finish(slot, out):
        arrive(rec_d.at[slot], d_send.at[slot], d_recv.at[slot], ens, E, by_ens)
        for e in range(E):
            out[e * piece : (e + 1) * piece, :] = rec_d[slot, e]

    sent = []
    stash(0, dot(gated[...], back[...], ((0,), (0,))))
    sent += start_a(0)
    stash(1, dot(gated_back[...], normed[...], ((0,), (0,))))
    sent += start_a(1)
    sent += start_b(0)

    out_grad = dot(flows[...], resid[...], ((1,), (0,)))
    chunk = SMALL_ROWS // (2 * E)

    def put(row, value):
        done = 0
        count = value.shape[0]
        while done < count:
            block, offset = divmod(row + done, chunk)
            take = min(count - done, chunk - offset)
            small[block, offset : offset + take, :] = value[done : done + take]
            done += take

    put(0, out_grad[:GRAD_ROW])

    upper[:, 0:channels] = dot(gated_back[...], up, ((1,), (0,)))
    gain_sum = jnp.zeros((1, channels), F32)
    for i in range(slab):
        back_norm = upper[i * zonal : (i + 1) * zonal, 0:channels]
        scaled = scaled_s[i]
        gain_sum = gain_sum + jnp.sum(back_norm * scaled, axis=0, keepdims=True)
        g = back_norm * gain[...]
        depth[i] = inv_s[i] * (
            g
            - jnp.mean(g, axis=-1, keepdims=True)
            - scaled * jnp.mean(g * scaled, axis=-1, keepdims=True)
        )
    sent += start_b(1)

    lane = 32

    def tap_columns(b, carry):
        sums = [jnp.zeros((8, channels), F32) for _ in range(SIDE)]
        for base in range(0, zonal, lane):
            g = [depth[i, base : base + lane, :] for i in range(slab)]
            wides = [jnp.zeros((lane, channels), F32)] * SIDE
            for r in range(2 * HALF + slab):
                x = wide[r, pl.ds(base + PAD - HALF + b, lane), :]
                for i in range(slab):
                    a = r - i
                    if 0 <= a < SIDE:
                        wides[a] = wides[a] + g[i] * x
            for a in range(SIDE):
                sums[a] = sums[a] + jnp.sum(wides[a].reshape(lane // 8, 8, channels), axis=0)
        for a in range(SIDE):
            tap_grad[pl.ds(a * SIDE + b, 1), :] = jnp.sum(sums[a], axis=0, keepdims=True)
        return carry

    lax.fori_loop(0, 4, tap_columns, 0)
    sent += start_c(0)
    lax.fori_loop(4, SIDE, tap_columns, 0)
    put(GRAD_ROW, tap_grad[...])
    tail = GRAD_ROW + SIDE * SIDE
    put(tail, gain_sum)
    put(tail + 1, jnp.broadcast_to(loss, (1, channels)))
    put(tail + 2, jnp.zeros((SMALL_ROWS - tail - 2, channels), F32))

    plane = ens * 2 + core

    def by_plane(o):
        return at(o // 2, z * 2 + o % 2)

    small_b[pl.ds(plane, 1)] = small[pl.ds(plane, 1)]
    sent += scatter(lambda o: small.at[o], small_b, p_send, p_recv, plane, 2 * E, by_plane)
    sent += start_c(1)
    sent += start_d(0)
    arrive(small_b, p_send, p_recv, plane, 2 * E, by_plane)
    total = small_b[0]
    for o in range(1, 2 * E):
        total = total + small_b[o]
    small_pc[...] = total
    small_c[pl.ds(z, 1)] = total[None]
    sent += scatter(lambda o: small_pc, small_c, q_send, q_recv, z, Z, by_z)
    sent += start_d(1)
    arrive(small_c, q_send, q_recv, z, Z, by_z)
    total = small_c[0]
    for o in range(1, Z):
        total = total + small_c[o]
    small_d[pl.ds(plane, 1)] = total[None]
    sent += scatter(lambda o: small_d.at[plane], small_d, r_send, r_recv, plane, 2 * E, by_plane)
    finish(0, down_o)
    finish(1, up_o)
    arrive(small_d, r_send, r_recv, plane, 2 * E, by_plane)
    final = jnp.concatenate([small_d[o] for o in range(2 * E)], axis=0)
    out_o[...] = final[:quantities]
    taps_o[...] = final[GRAD_ROW:tail]
    gain_o[...] = final[tail : tail + 1]
    crps_o[...] = final[tail + 1 : tail + 2, 0:1]

    for copy in own + forwards + shares + sent:
        copy.wait_send()

    @pl.when(lat < L - 1)
    def _():
        south.wait_send()

    @pl.when(lat > 0)
    def _():
        north.wait_send()


def finish_kernel(*refs):
    count = (len(refs) - 1) // 2
    copies = [
        pltpu.make_async_copy(refs[n], refs[count + n], refs[-1].at[n]) for n in range(count)
    ]
    for copy in copies:
        copy.start()
    for copy in copies:
        copy.wait()


def on_device(
    features, random_perturbation, observed_truth, stencil_taps,
    affine_factor, widen_matrix, shrink_matrix, readout_matrix,
):
    E, L = lax.axis_size("ens"), lax.axis_size("lat")
    Z = L // 2
    _, slab, zonal, channels = random_perturbation.shape
    quantities = readout_matrix.shape[0]
    unit = widen_matrix.shape[0]
    hidden = unit * L
    piece = unit // E
    points = slab * zonal
    rows = -(-quantities // 16) * 16
    chunk = SMALL_ROWS // (2 * E)
    vmem = pl.BlockSpec(memory_space=pltpu.VMEM)
    dma = pltpu.SemaphoreType.DMA
    out = jax.ShapeDtypeStruct
    hbm = pl.BlockSpec(memory_space=pltpu.HBM)
    grid = (1, quantities, slab, zonal)
    shapes = [
        out((1, 1), F32),
        out((SIDE * SIDE, channels), F32),
        out((1, channels), F32),
        out((unit, channels), F32),
        out((unit, channels), F32),
        out((quantities, channels), F32),
        out(grid, BF16),
        out(grid, F32),
    ]
    results = pl.pallas_call(
        functools.partial(kernel, (E, L)),
        out_shape=shapes,
        in_specs=[hbm] * 8,
        out_specs=[vmem] * 8,
        scratch_shapes=[
            pltpu.VMEM((slab, zonal, channels), BF16),
            pltpu.VMEM((1, slab, zonal, channels), BF16),
            pltpu.VMEM((quantities, slab, zonal), F32),
            pltpu.VMEM((SIDE * SIDE, channels), F32),
            pltpu.VMEM((1, channels), F32),
            pltpu.VMEM((quantities, channels), BF16),
            pltpu.VMEM((slab + 2 * HALF, zonal, channels), BF16),
            pltpu.VMEM((slab + 2 * HALF, zonal + 2 * PAD, channels), F32),
            pltpu.VMEM((SIDE * SIDE, 8, channels), F32),
            pltpu.VMEM((slab, zonal, channels), F32),
            pltpu.VMEM((slab, zonal, channels), F32),
            pltpu.VMEM((slab, zonal, channels), F32),
            pltpu.VMEM((points, channels), BF16),
            pltpu.VMEM((points, hidden), F32),
            pltpu.VMEM((points, hidden), F32),
            pltpu.VMEM((points, hidden), BF16),
            pltpu.VMEM((rows, channels), BF16),
            pltpu.VMEM((slab, E, rows, zonal), BF16),
            pltpu.VMEM((L, 2, unit, channels), BF16),
            pltpu.VMEM((points, channels), BF16),
            pltpu.VMEM((rows, points), BF16),
            pltpu.VMEM((points, channels), BF16),
            pltpu.VMEM((points, hidden), BF16),
            pltpu.VMEM((rows, slab, zonal), F32),
            pltpu.VMEM((SIDE * SIDE, channels), F32),
            pltpu.VMEM((2, 2, E, Z, piece, channels), F32),
            pltpu.VMEM((2, E, Z, piece, channels), F32),
            pltpu.VMEM((2, E, Z, piece, channels), F32),
            pltpu.VMEM((2, E, Z, piece, channels), F32),
            pltpu.VMEM((2, Z, piece, channels), F32),
            pltpu.VMEM((2, Z, piece, channels), F32),
            pltpu.VMEM((2, E, piece, channels), F32),
            pltpu.VMEM((2 * E, chunk, channels), F32),
            pltpu.VMEM((2 * E, chunk, channels), F32),
            pltpu.VMEM((chunk, channels), F32),
            pltpu.VMEM((Z, chunk, channels), F32),
            pltpu.VMEM((2 * E, chunk, channels), F32),
            dma((8,)), dma((2,)), dma((2,)),
            dma((Z,)), dma((Z,)), dma((L,)),
            dma((slab, E)), dma((slab, E)),
            dma((2,)), dma((2,)),
            dma((2, E)), dma((2, E)),
            dma((2, Z)), dma((2, Z)),
            dma((2, E)), dma((2, E)),
            dma((2 * E,)), dma((2 * E,)),
            dma((Z,)), dma((Z,)),
            dma((2 * E,)), dma((2 * E,)),
        ],
        compiler_params=pltpu.CompilerParams(
            collective_id=0, has_side_effects=True, vmem_limit_bytes=40 * 1024 * 1024
        ),
        cost_estimate=pl.CostEstimate(
            flops=12 * points * channels * hidden, bytes_accessed=2_000_000, transcendentals=0
        ),
    )(
        features, random_perturbation, observed_truth, stencil_taps,
        affine_factor.reshape(1, channels), widen_matrix, shrink_matrix, readout_matrix,
    )
    anywhere = pl.BlockSpec(memory_space=pl.ANY)
    crps, taps, gain, up, down, head, look, spread = pl.pallas_call(
        finish_kernel,
        out_shape=shapes,
        in_specs=[anywhere] * 8,
        out_specs=[hbm] * 8,
        scratch_shapes=[dma((8,))],
    )(*results)
    return (
        crps.reshape(()), taps, gain.reshape(channels), up, down, head, look, spread,
    )


def solution(mesh):
    in_specs = (
        P("lat", None, None),
        P("ens", "lat", None, None),
        P(None, "lat", None),
        P(),
        P(),
        P("lat", None),
        P("lat", None),
        P(),
    )
    out_specs = (
        P(),
        P(),
        P(),
        P("lat", None),
        P("lat", None),
        P(),
        P("ens", None, "lat", None),
        P("ens", None, "lat", None),
    )
    return jax.shard_map(
        on_device, mesh=mesh, in_specs=in_specs, out_specs=out_specs, check_vma=False
    )
```

```python
import functools
import math

import jax
import jax.numpy as jnp
from jax import lax
from jax.experimental import pallas as pl
from jax.experimental.pallas import tpu as pltpu
from jax.sharding import PartitionSpec as P

SIDE = 7
HALF = SIDE // 2
SQRT_TWO_PI = 0.7978845608028654
CUBIC = 0.044715
EPSILON = 1e-06
SMOOTHING = 0.01
PAD = 8
GRAD_ROW = 72
SMALL_ROWS = 128
F32 = jnp.float32
BF16 = jnp.bfloat16


def dot(a, b, dims):
    return lax.dot_general(a, b, (dims, ((), ())), preferred_element_type=F32)


def kernel(
    sizes,
    feat_h, noise_h, obs_h, taps_h, gain_h, widen_h, shrink_h, readout_h,
    crps_o, taps_o, gain_o, up_o, down_o, out_o, look_o, spread_o,
    feat, noise, obs, taps, gain, readout,
    ext, wide, tapb, depth, scaled_s, inv_s, normed, upper, inner, gated, ro, looks, wbuf,
    resid, flows, back, gated_back, outlook, tap_grad,
    grads, rec_a, part_b, rec_b, part_c, rec_c, rec_d,
    small, small_b, small_pc, small_c, small_d,
    in_sem, halo_send, halo_recv, w_send, w_fwd, w_recv, e_send, e_recv,
    a_send, a_recv, b_send, b_recv, c_send, c_recv, d_send, d_recv,
    p_send, p_recv, q_send, q_recv, r_send, r_recv,
):
    E, L = sizes
    Z = L // 2
    slab, zonal, channels = feat.shape
    quantities = obs.shape[0]
    rows = ro.shape[0]
    points = slab * zonal
    hidden = L * wbuf.shape[2]
    piece = wbuf.shape[2] // E
    ens = lax.axis_index("ens")
    lat = lax.axis_index("lat")
    z = lat // 2
    core = lat % 2
    sibling = z * 2 + (1 - core)

    def at(e, l):
        return {"ens": e, "lat": l}

    def remote(src, dst, send, recv, where):
        return pltpu.make_async_remote_copy(
            src_ref=src, dst_ref=dst, send_sem=send, recv_sem=recv,
            device_id=where, device_id_type=pl.DeviceIdType.MESH,
        )

    barrier = pltpu.get_barrier_semaphore()
    for k in range(1, L):
        pl.semaphore_signal(barrier, inc=1, device_id=at(ens, (lat + k) % L),
                            device_id_type=pl.DeviceIdType.MESH)
    for k in range(1, E):
        for l in (lat, sibling):
            pl.semaphore_signal(barrier, inc=1, device_id=at((ens + k) % E, l),
                                device_id_type=pl.DeviceIdType.MESH)

    loads = [
        pltpu.make_async_copy(src, dst, in_sem.at[n])
        for n, (src, dst) in enumerate([
            (feat_h, feat), (noise_h, noise), (widen_h, wbuf.at[lat, 0]),
            (shrink_h, wbuf.at[lat, 1]), (taps_h, taps), (readout_h, readout),
            (gain_h, gain), (obs_h, obs),
        ])
    ]
    for copy in loads:
        copy.start()

    def widen_rows(start, count):
        block = ext[start : start + count].astype(F32)
        wide[start : start + count, PAD : PAD + zonal, :] = block
        wide[start : start + count, 0:PAD, :] = block[:, zonal - PAD :, :]
        wide[start : start + count, PAD + zonal :, :] = block[:, :PAD, :]

    loads[0].wait()
    loads[1].wait()
    field = (feat[...].astype(F32) + noise[0].astype(F32)).astype(BF16)
    ext[HALF : HALF + slab] = field
    pl.semaphore_wait(barrier, L - 1 + 2 * (E - 1))

    south = remote(ext.at[pl.ds(slab, HALF)], ext.at[pl.ds(0, HALF)],
                   halo_send.at[0], halo_recv.at[0], at(ens, jnp.minimum(lat + 1, L - 1)))
    north = remote(ext.at[pl.ds(HALF, HALF)], ext.at[pl.ds(HALF + slab, HALF)],
                   halo_send.at[1], halo_recv.at[1], at(ens, jnp.maximum(lat - 1, 0)))

    @pl.when(lat < L - 1)
    def _():
        south.start()

    @pl.when(lat > 0)
    def _():
        north.start()

    own = [
        remote(wbuf.at[lat], wbuf.at[lat], w_send.at[k], w_recv.at[lat],
               at(ens, ((z + k) % Z) * 2 + core))
        for k in range(1, Z)
    ]
    loads[2].wait()
    loads[3].wait()
    for copy in own:
        copy.start()
    forwards = [remote(wbuf.at[lat], wbuf.at[lat], w_fwd.at[0], w_recv.at[lat], at(ens, sibling))]
    forwards[0].start()

    widen_rows(HALF, slab)
    for copy in loads[4:]:
        copy.wait()
    for t in range(SIDE * SIDE):
        tapb[t] = jnp.broadcast_to(taps[t : t + 1, :], (8, channels))
    ro[...] = jnp.zeros_like(ro)
    ro[0:quantities, :] = readout[...]

    step = 32

    def convolve(ext_rows, fresh):
        def body(t, carry):
            base = pl.multiple_of(t * step, step)
            sums = []
            for i in range(slab):
                if fresh:
                    sums.append(jnp.zeros((step // 8, 8, channels), F32))
                else:
                    sums.append(depth[i, pl.ds(base, step), :].reshape(step // 8, 8, channels))
            for b in range(SIDE):
                for r in ext_rows:
                    x = wide[r, pl.ds(base + PAD - HALF + b, step), :].reshape(
                        step // 8, 8, channels)
                    for i in range(slab):
                        a = r - i
                        if 0 <= a < SIDE:
                            sums[i] = sums[i] + tapb[a * SIDE + b] * x
            for i in range(slab):
                depth[i, pl.ds(base, step), :] = sums[i].reshape(step, channels)
            return carry

        lax.fori_loop(0, zonal // step, body, 0)

    convolve(range(HALF, HALF + slab), True)

    for k in range(1, Z):
        other = ((z + k) % Z) * 2 + core
        remote(wbuf.at[other], wbuf.at[other], w_send.at[k], w_recv.at[other],
               at(ens, other)).wait_recv()
        copy = remote(wbuf.at[other], wbuf.at[other], w_fwd.at[k], w_recv.at[other],
                      at(ens, sibling))
        copy.start()
        forwards.append(copy)

    @pl.when(lat > 0)
    def _():
        south.wait_recv()
        widen_rows(0, HALF)

    @pl.when(lat == 0)
    def _():
        wide[0:HALF] = jnp.zeros((HALF, zonal + 2 * PAD, channels), F32)

    @pl.when(lat < L - 1)
    def _():
        north.wait_recv()
        widen_rows(HALF + slab, HALF)

    @pl.when(lat == L - 1)
    def _():
        wide[HALF + slab :] = jnp.zeros((HALF, zonal + 2 * PAD, channels), F32)

    convolve([*range(HALF), *range(HALF + slab, 2 * HALF + slab)], False)

    for i in range(slab):
        d = depth[i]
        centred = d - jnp.mean(d, axis=-1, keepdims=True)
        inverse = lax.rsqrt(jnp.mean(centred * centred, axis=-1, keepdims=True) + EPSILON)
        scaled = centred * inverse
        scaled_s[i] = scaled
        inv_s[i] = jnp.broadcast_to(inverse, (zonal, channels))
        normed[i * zonal : (i + 1) * zonal, :] = (gain[...] * scaled).astype(BF16)

    for k in range(Z):
        other = ((z + k) % Z) * 2 + (1 - core)
        remote(wbuf.at[other], wbuf.at[other], w_fwd.at[k], w_recv.at[other],
               at(ens, sibling)).wait_recv()

    up = wbuf[:, 0].reshape(hidden, channels)
    down = wbuf[:, 1].reshape(hidden, channels)
    sub = 32
    shares = []
    for i in range(slab):
        begin, end = i * zonal, (i + 1) * zonal
        upper[begin:end, :] = dot(normed[begin:end, :], up, ((1,), (1,)))
        for t in range(begin, end, sub):
            u = upper[t : t + sub, :]
            th = jnp.tanh(SQRT_TWO_PI * (u + CUBIC * u * u * u))
            inner[t : t + sub, :] = th
            gated[t : t + sub, :] = (0.5 * u * (1.0 + th)).astype(BF16)
        mixed = dot(gated[begin:end, :], down, ((1,), (0,)))
        residual = (ext[HALF + i].astype(F32) + mixed).astype(BF16)
        resid[begin:end, :] = residual
        mine = dot(ro[...], residual, ((1,), (1,))).astype(BF16)
        looks[i, pl.ds(ens, 1)] = mine[None]
        for k in range(1, E):
            copy = remote(looks.at[i, ens], looks.at[i, ens], e_send.at[i, k], e_recv.at[i, ens],
                          at((ens + k) % E, lat))
            copy.start()
            shares.append(copy)
        outlook[:, i, :] = mine.astype(F32)

    look_o[0] = outlook[0:quantities].astype(BF16)

    for t in range(0, points, sub):
        u = upper[t : t + sub, :]
        th = inner[t : t + sub, :]
        inner[t : t + sub, :] = 0.5 * (1.0 + th) + 0.5 * u * (1.0 - th * th) * SQRT_TWO_PI * (
            1.0 + 3.0 * CUBIC * u * u
        )

    members = E
    pair_norm = 1.0 / (members * (members - 1))
    latitudes = slab * L
    loss = jnp.zeros((1, channels), F32)
    for i in range(slab):
        begin, end = i * zonal, (i + 1) * zonal
        row = jnp.full((8, zonal), lat * slab + i, jnp.int32).astype(F32)
        area = jnp.cos(math.pi * ((row + 0.5) / latitudes - 0.5))
        weight = (area * (1.0 / (latitudes * zonal)))[0:1]
        mine = looks[i, pl.ds(ens, 1)][0].astype(F32)
        truth = jnp.concatenate(
            [obs[:, i, :], jnp.zeros((rows - quantities, zonal), F32)], axis=0)
        miss = mine - truth
        square = miss * miss + SMOOTHING
        root = lax.rsqrt(square)
        miss_size = square * root
        miss_slope = miss * root
        spread = jnp.full((rows, zonal), math.sqrt(SMOOTHING), F32)
        ranks = jnp.zeros((rows, zonal), F32)
        for k in range(1, E):
            other = (ens + k) % E
            remote(looks.at[i, other], looks.at[i, other], e_send.at[i, k], e_recv.at[i, other],
                   at(other, lat)).wait_recv()
            gap = mine - looks[i, pl.ds(other, 1)][0].astype(F32)
            square = gap * gap + SMOOTHING
            root = lax.rsqrt(square)
            spread = spread + square * root
            ranks = ranks + gap * root
        spread_o[0, :, i, :] = spread[:quantities] * (1.0 / (members - 1))
        part = weight * (miss_size / members - 0.5 * pair_norm * spread)
        loss = loss + jnp.sum(part[:quantities], axis=0, keepdims=True)
        flow = (weight * (miss_slope / members - pair_norm * ranks)).astype(BF16)
        flows[:, begin:end] = flow
        back_residual = dot(flow, ro[...], ((0,), (0,))).astype(BF16)
        back[begin:end, :] = back_residual
        upper[begin:end, :] = dot(back_residual, down, ((1,), (1,)))
        for t in range(begin, end, sub):
            gated_back[t : t + sub, :] = (
                upper[t : t + sub, :] * inner[t : t + sub, :]).astype(BF16)
    loss = jnp.sum(loss, axis=1, keepdims=True)

    def stash(slot, value):
        for l in range(L):
            for e in range(E):
                begin = (l * E + e) * piece
                grads[slot, l % 2, e, l // 2] = value[begin : begin + piece]

    def start_a(slot):
        copy = remote(grads.at[slot, 1 - core], rec_a.at[slot], a_send.at[slot], a_recv.at[slot],
                      at(ens, sibling))
        copy.start()
        return [copy]

    def scatter(src, dst, send, recv, me, count, place):
        copies = [
            remote(src((me + k) % count), dst.at[me], send.at[k], recv.at[me],
                   place((me + k) % count))
            for k in range(1, count)
        ]
        for copy in copies:
            copy.start()
        return copies

    def arrive(dst, send, recv, me, count, place):
        for k in range(1, count):
            other = (me + k) % count
            remote(dst.at[other], dst.at[other], send.at[k], recv.at[other],
                   place(other)).wait_recv()

    def by_ens(e):
        return at(e, lat)

    def by_z(other):
        return at(ens, other * 2 + core)

    def start_b(slot):
        sent = remote(grads.at[slot, 1 - core], rec_a.at[slot], a_send.at[slot], a_recv.at[slot],
                      at(ens, sibling))
        sent.wait_recv()
        part_b[slot] = grads[slot, pl.ds(core, 1)][0] + rec_a[slot]
        rec_b[slot, pl.ds(ens, 1)] = part_b[slot, pl.ds(ens, 1)]
        return scatter(lambda e: part_b.at[slot, e], rec_b.at[slot], b_send.at[slot],
                       b_recv.at[slot], ens, E, by_ens)

    def start_c(slot):
        arrive(rec_b.at[slot], b_send.at[slot], b_recv.at[slot], ens, E, by_ens)
        total = rec_b[slot, 0]
        for e in range(1, E):
            total = total + rec_b[slot, e]
        part_c[slot] = total
        rec_c[slot, pl.ds(z, 1)] = part_c[slot, pl.ds(z, 1)]
        return scatter(lambda o: part_c.at[slot, o], rec_c.at[slot], c_send.at[slot],
                       c_recv.at[slot], z, Z, by_z)

    def start_d(slot):
        arrive(rec_c.at[slot], c_send.at[slot], c_recv.at[slot], z, Z, by_z)
        total = rec_c[slot, 0]
        for o in range(1, Z):
            total = total + rec_c[slot, o]
        rec_d[slot, pl.ds(ens, 1)] = total[None]
        return scatter(lambda e: rec_d.at[slot, ens], rec_d.at[slot], d_send.at[slot],
                       d_recv.at[slot], ens, E, by_ens)

    def finish(slot, out):
        arrive(rec_d.at[slot], d_send.at[slot], d_recv.at[slot], ens, E, by_ens)
        for e in range(E):
            out[e * piece : (e + 1) * piece, :] = rec_d[slot, e]

    sent = []
    stash(0, dot(gated[...], back[...], ((0,), (0,))))
    sent += start_a(0)
    stash(1, dot(gated_back[...], normed[...], ((0,), (0,))))
    sent += start_a(1)
    sent += start_b(0)

    out_grad = dot(flows[...], resid[...], ((1,), (0,)))
    chunk = SMALL_ROWS // (2 * E)

    def put(row, value):
        done = 0
        count = value.shape[0]
        while done < count:
            block, offset = divmod(row + done, chunk)
            take = min(count - done, chunk - offset)
            small[block, offset : offset + take, :] = value[done : done + take]
            done += take

    put(0, out_grad[:GRAD_ROW])

    upper[:, 0:channels] = dot(gated_back[...], up, ((1,), (0,)))
    gain_sum = jnp.zeros((1, channels), F32)
    for i in range(slab):
        back_norm = upper[i * zonal : (i + 1) * zonal, 0:channels]
        scaled = scaled_s[i]
        gain_sum = gain_sum + jnp.sum(back_norm * scaled, axis=0, keepdims=True)
        g = back_norm * gain[...]
        depth[i] = inv_s[i] * (
            g
            - jnp.mean(g, axis=-1, keepdims=True)
            - scaled * jnp.mean(g * scaled, axis=-1, keepdims=True)
        )
    sent += start_b(1)

    lane = 32

    def tap_columns(b, carry):
        sums = [jnp.zeros((8, channels), F32) for _ in range(SIDE)]
        for base in range(0, zonal, lane):
            g = [depth[i, base : base + lane, :] for i in range(slab)]
            wides = [jnp.zeros((lane, channels), F32)] * SIDE
            for r in range(2 * HALF + slab):
                x = wide[r, pl.ds(base + PAD - HALF + b, lane), :]
                for i in range(slab):
                    a = r - i
                    if 0 <= a < SIDE:
                        wides[a] = wides[a] + g[i] * x
            for a in range(SIDE):
                sums[a] = sums[a] + jnp.sum(wides[a].reshape(lane // 8, 8, channels), axis=0)
        for a in range(SIDE):
            tap_grad[pl.ds(a * SIDE + b, 1), :] = jnp.sum(sums[a], axis=0, keepdims=True)
        return carry

    lax.fori_loop(0, 4, tap_columns, 0)
    sent += start_c(0)
    lax.fori_loop(4, SIDE, tap_columns, 0)
    put(GRAD_ROW, tap_grad[...])
    tail = GRAD_ROW + SIDE * SIDE
    put(tail, gain_sum)
    put(tail + 1, jnp.broadcast_to(loss, (1, channels)))
    put(tail + 2, jnp.zeros((SMALL_ROWS - tail - 2, channels), F32))

    plane = ens * 2 + core

    def by_plane(o):
        return at(o // 2, z * 2 + o % 2)

    small_b[pl.ds(plane, 1)] = small[pl.ds(plane, 1)]
    sent += scatter(lambda o: small.at[o], small_b, p_send, p_recv, plane, 2 * E, by_plane)
    sent += start_c(1)
    sent += start_d(0)
    arrive(small_b, p_send, p_recv, plane, 2 * E, by_plane)
    total = small_b[0]
    for o in range(1, 2 * E):
        total = total + small_b[o]
    small_pc[...] = total
    small_c[pl.ds(z, 1)] = total[None]
    sent += scatter(lambda o: small_pc, small_c, q_send, q_recv, z, Z, by_z)
    sent += start_d(1)
    arrive(small_c, q_send, q_recv, z, Z, by_z)
    total = small_c[0]
    for o in range(1, Z):
        total = total + small_c[o]
    small_d[pl.ds(plane, 1)] = total[None]
    sent += scatter(lambda o: small_d.at[plane], small_d, r_send, r_recv, plane, 2 * E, by_plane)
    finish(0, down_o)
    finish(1, up_o)
    arrive(small_d, r_send, r_recv, plane, 2 * E, by_plane)
    final = jnp.concatenate([small_d[o] for o in range(2 * E)], axis=0)
    out_o[...] = final[:quantities]
    taps_o[...] = final[GRAD_ROW:tail]
    gain_o[...] = final[tail : tail + 1]
    crps_o[...] = final[tail + 1 : tail + 2, 0:1]

    for copy in own + forwards + shares + sent:
        copy.wait_send()

    @pl.when(lat < L - 1)
    def _():
        south.wait_send()

    @pl.when(lat > 0)
    def _():
        north.wait_send()


def finish_kernel(*refs):
    count = (len(refs) - 1) // 2
    copies = [
        pltpu.make_async_copy(refs[n], refs[count + n], refs[-1].at[n]) for n in range(count)
    ]
    for copy in copies:
        copy.start()
    for copy in copies:
        copy.wait()


def on_device(
    features, random_perturbation, observed_truth, stencil_taps,
    affine_factor, widen_matrix, shrink_matrix, readout_matrix,
):
    E, L = lax.axis_size("ens"), lax.axis_size("lat")
    Z = L // 2
    _, slab, zonal, channels = random_perturbation.shape
    quantities = readout_matrix.shape[0]
    unit = widen_matrix.shape[0]
    hidden = unit * L
    piece = unit // E
    points = slab * zonal
    rows = -(-quantities // 16) * 16
    chunk = SMALL_ROWS // (2 * E)
    vmem = pl.BlockSpec(memory_space=pltpu.VMEM)
    dma = pltpu.SemaphoreType.DMA
    out = jax.ShapeDtypeStruct
    hbm = pl.BlockSpec(memory_space=pltpu.HBM)
    grid = (1, quantities, slab, zonal)
    shapes = [
        out((1, 1), F32),
        out((SIDE * SIDE, channels), F32),
        out((1, channels), F32),
        out((unit, channels), F32),
        out((unit, channels), F32),
        out((quantities, channels), F32),
        out(grid, BF16),
        out(grid, F32),
    ]
    results = pl.pallas_call(
        functools.partial(kernel, (E, L)),
        out_shape=shapes,
        in_specs=[hbm] * 8,
        out_specs=[vmem] * 8,
        scratch_shapes=[
            pltpu.VMEM((slab, zonal, channels), BF16),
            pltpu.VMEM((1, slab, zonal, channels), BF16),
            pltpu.VMEM((quantities, slab, zonal), F32),
            pltpu.VMEM((SIDE * SIDE, channels), F32),
            pltpu.VMEM((1, channels), F32),
            pltpu.VMEM((quantities, channels), BF16),
            pltpu.VMEM((slab + 2 * HALF, zonal, channels), BF16),
            pltpu.VMEM((slab + 2 * HALF, zonal + 2 * PAD, channels), F32),
            pltpu.VMEM((SIDE * SIDE, 8, channels), F32),
            pltpu.VMEM((slab, zonal, channels), F32),
            pltpu.VMEM((slab, zonal, channels), F32),
            pltpu.VMEM((slab, zonal, channels), F32),
            pltpu.VMEM((points, channels), BF16),
            pltpu.VMEM((points, hidden), F32),
            pltpu.VMEM((points, hidden), F32),
            pltpu.VMEM((points, hidden), BF16),
            pltpu.VMEM((rows, channels), BF16),
            pltpu.VMEM((slab, E, rows, zonal), BF16),
            pltpu.VMEM((L, 2, unit, channels), BF16),
            pltpu.VMEM((points, channels), BF16),
            pltpu.VMEM((rows, points), BF16),
            pltpu.VMEM((points, channels), BF16),
            pltpu.VMEM((points, hidden), BF16),
            pltpu.VMEM((rows, slab, zonal), F32),
            pltpu.VMEM((SIDE * SIDE, channels), F32),
            pltpu.VMEM((2, 2, E, Z, piece, channels), F32),
            pltpu.VMEM((2, E, Z, piece, channels), F32),
            pltpu.VMEM((2, E, Z, piece, channels), F32),
            pltpu.VMEM((2, E, Z, piece, channels), F32),
            pltpu.VMEM((2, Z, piece, channels), F32),
            pltpu.VMEM((2, Z, piece, channels), F32),
            pltpu.VMEM((2, E, piece, channels), F32),
            pltpu.VMEM((2 * E, chunk, channels), F32),
            pltpu.VMEM((2 * E, chunk, channels), F32),
            pltpu.VMEM((chunk, channels), F32),
            pltpu.VMEM((Z, chunk, channels), F32),
            pltpu.VMEM((2 * E, chunk, channels), F32),
            dma((8,)), dma((2,)), dma((2,)),
            dma((Z,)), dma((Z,)), dma((L,)),
            dma((slab, E)), dma((slab, E)),
            dma((2,)), dma((2,)),
            dma((2, E)), dma((2, E)),
            dma((2, Z)), dma((2, Z)),
            dma((2, E)), dma((2, E)),
            dma((2 * E,)), dma((2 * E,)),
            dma((Z,)), dma((Z,)),
            dma((2 * E,)), dma((2 * E,)),
        ],
        compiler_params=pltpu.CompilerParams(
            collective_id=0, has_side_effects=True, vmem_limit_bytes=40 * 1024 * 1024
        ),
        cost_estimate=pl.CostEstimate(
            flops=12 * points * channels * hidden, bytes_accessed=2_000_000, transcendentals=0
        ),
    )(
        *[
            pltpu.with_memory_space_constraint(value, pltpu.HBM)
            for value in (
                features, random_perturbation, observed_truth, stencil_taps,
                affine_factor.reshape(1, channels), widen_matrix, shrink_matrix, readout_matrix,
            )
        ]
    )
    crps, taps, gain, up, down, head, look, spread = pl.pallas_call(
        finish_kernel,
        out_shape=shapes,
        in_specs=[vmem] * 8,
        out_specs=[hbm] * 8,
        scratch_shapes=[dma((8,))],
        compiler_params=pltpu.CompilerParams(vmem_limit_bytes=8 * 1024 * 1024),
    )(*results)
    return (
        crps.reshape(()), taps, gain.reshape(channels), up, down, head, look, spread,
    )


def solution(mesh):
    in_specs = (
        P("lat", None, None),
        P("ens", "lat", None, None),
        P(None, "lat", None),
        P(),
        P(),
        P("lat", None),
        P("lat", None),
        P(),
    )
    out_specs = (
        P(),
        P(),
        P(),
        P("lat", None),
        P("lat", None),
        P(),
        P("ens", None, "lat", None),
        P("ens", None, "lat", None),
    )
    return jax.shard_map(
        on_device, mesh=mesh, in_specs=in_specs, out_specs=out_specs, check_vma=False
    )
```

```python
import functools
import math

import jax
import jax.numpy as jnp
from jax import lax
from jax.experimental import pallas as pl
from jax.experimental.pallas import tpu as pltpu
from jax.sharding import PartitionSpec as P

SIDE = 7
HALF = SIDE // 2
SQRT_TWO_PI = 0.7978845608028654
CUBIC = 0.044715
EPSILON = 1e-06
SMOOTHING = 0.01
PAD = 8
GRAD_ROW = 72
SMALL_ROWS = 128
F32 = jnp.float32
BF16 = jnp.bfloat16


def dot(a, b, dims):
    return lax.dot_general(a, b, (dims, ((), ())), preferred_element_type=F32)


def kernel(
    sizes,
    feat_h, noise_h, obs_h, taps_h, gain_h, widen_h, shrink_h, readout_h,
    crps_o, taps_o, gain_o, up_o, down_o, out_o, look_o, spread_o,
    feat, noise, obs, taps, gain, readout,
    ext, wide, tapb, depth, scaled_s, inv_s, normed, upper, inner, gated, ro, looks, wbuf,
    resid, flows, back, gated_back, outlook, truths, tap_grad,
    grads, rec_a, part_b, rec_b, part_c, rec_c, rec_d,
    small, small_b, small_pc, small_c, small_d,
    in_sem, halo_send, halo_recv, w_send, w_fwd, w_recv, e_send, e_recv,
    a_send, a_recv, b_send, b_recv, c_send, c_recv, d_send, d_recv,
    p_send, p_recv, q_send, q_recv, r_send, r_recv,
):
    E, L = sizes
    Z = L // 2
    slab, zonal, channels = feat.shape
    quantities = obs.shape[0]
    rows = ro.shape[0]
    points = slab * zonal
    hidden = L * wbuf.shape[2]
    piece = wbuf.shape[2] // E
    ens = lax.axis_index("ens")
    lat = lax.axis_index("lat")
    z = lat // 2
    core = lat % 2
    sibling = z * 2 + (1 - core)

    def at(e, l):
        return {"ens": e, "lat": l}

    def remote(src, dst, send, recv, where):
        return pltpu.make_async_remote_copy(
            src_ref=src, dst_ref=dst, send_sem=send, recv_sem=recv,
            device_id=where, device_id_type=pl.DeviceIdType.MESH,
        )

    barrier = pltpu.get_barrier_semaphore()
    for k in range(1, L):
        pl.semaphore_signal(barrier, inc=1, device_id=at(ens, (lat + k) % L),
                            device_id_type=pl.DeviceIdType.MESH)
    for k in range(1, E):
        for l in (lat, sibling):
            pl.semaphore_signal(barrier, inc=1, device_id=at((ens + k) % E, l),
                                device_id_type=pl.DeviceIdType.MESH)

    loads = [
        pltpu.make_async_copy(src, dst, in_sem.at[n])
        for n, (src, dst) in enumerate([
            (feat_h, feat), (noise_h, noise), (widen_h, wbuf.at[lat, 0]),
            (shrink_h, wbuf.at[lat, 1]), (taps_h, taps), (readout_h, readout),
            (gain_h, gain), (obs_h, obs),
        ])
    ]
    for copy in loads:
        copy.start()

    def widen_rows(start, count):
        block = ext[start : start + count].astype(F32)
        wide[start : start + count, PAD : PAD + zonal, :] = block
        wide[start : start + count, 0:PAD, :] = block[:, zonal - PAD :, :]
        wide[start : start + count, PAD + zonal :, :] = block[:, :PAD, :]

    pl.semaphore_wait(barrier, L - 1 + 2 * (E - 1))
    loads[2].wait()
    loads[3].wait()
    own = [
        remote(wbuf.at[lat], wbuf.at[lat], w_send.at[k], w_recv.at[lat],
               at(ens, ((z + k) % Z) * 2 + core))
        for k in range(1, Z)
    ]
    for copy in own:
        copy.start()
    forwards = [remote(wbuf.at[lat], wbuf.at[lat], w_fwd.at[0], w_recv.at[lat], at(ens, sibling))]
    forwards[0].start()

    loads[0].wait()
    loads[1].wait()
    field = (feat[...].astype(F32) + noise[0].astype(F32)).astype(BF16)
    ext[HALF : HALF + slab] = field

    south = remote(ext.at[pl.ds(slab, HALF)], ext.at[pl.ds(0, HALF)],
                   halo_send.at[0], halo_recv.at[0], at(ens, jnp.minimum(lat + 1, L - 1)))
    north = remote(ext.at[pl.ds(HALF, HALF)], ext.at[pl.ds(HALF + slab, HALF)],
                   halo_send.at[1], halo_recv.at[1], at(ens, jnp.maximum(lat - 1, 0)))

    @pl.when(lat < L - 1)
    def _():
        south.start()

    @pl.when(lat > 0)
    def _():
        north.start()

    widen_rows(HALF, slab)
    for copy in loads[4:]:
        copy.wait()
    for t in range(SIDE * SIDE):
        tapb[t] = jnp.broadcast_to(taps[t : t + 1, :], (8, channels))
    ro[...] = jnp.zeros_like(ro)
    ro[0:quantities, :] = readout[...]

    step = 32

    def convolve(ext_rows, fresh):
        def body(t, carry):
            base = pl.multiple_of(t * step, step)
            sums = []
            for i in range(slab):
                if fresh:
                    sums.append(jnp.zeros((step // 8, 8, channels), F32))
                else:
                    sums.append(depth[i, pl.ds(base, step), :].reshape(step // 8, 8, channels))
            for b in range(SIDE):
                for r in ext_rows:
                    x = wide[r, pl.ds(base + PAD - HALF + b, step), :].reshape(
                        step // 8, 8, channels)
                    for i in range(slab):
                        a = r - i
                        if 0 <= a < SIDE:
                            sums[i] = sums[i] + tapb[a * SIDE + b] * x
            for i in range(slab):
                depth[i, pl.ds(base, step), :] = sums[i].reshape(step, channels)
            return carry

        lax.fori_loop(0, zonal // step, body, 0)

    convolve(range(HALF, HALF + slab), True)

    for k in range(1, Z):
        other = ((z + k) % Z) * 2 + core
        remote(wbuf.at[other], wbuf.at[other], w_send.at[k], w_recv.at[other],
               at(ens, other)).wait_recv()
        copy = remote(wbuf.at[other], wbuf.at[other], w_fwd.at[k], w_recv.at[other],
                      at(ens, sibling))
        copy.start()
        forwards.append(copy)

    @pl.when(lat > 0)
    def _():
        south.wait_recv()
        widen_rows(0, HALF)

    @pl.when(lat == 0)
    def _():
        wide[0:HALF] = jnp.zeros((HALF, zonal + 2 * PAD, channels), F32)

    @pl.when(lat < L - 1)
    def _():
        north.wait_recv()
        widen_rows(HALF + slab, HALF)

    @pl.when(lat == L - 1)
    def _():
        wide[HALF + slab :] = jnp.zeros((HALF, zonal + 2 * PAD, channels), F32)

    convolve([*range(HALF), *range(HALF + slab, 2 * HALF + slab)], False)

    for i in range(slab):
        d = depth[i]
        centred = d - jnp.mean(d, axis=-1, keepdims=True)
        inverse = lax.rsqrt(jnp.mean(centred * centred, axis=-1, keepdims=True) + EPSILON)
        scaled = centred * inverse
        scaled_s[i] = scaled
        inv_s[i] = jnp.broadcast_to(inverse, (zonal, channels))
        normed[i * zonal : (i + 1) * zonal, :] = (gain[...] * scaled).astype(BF16)

    for k in range(Z):
        other = ((z + k) % Z) * 2 + (1 - core)
        remote(wbuf.at[other], wbuf.at[other], w_fwd.at[k], w_recv.at[other],
               at(ens, sibling)).wait_recv()

    up = wbuf[:, 0].reshape(hidden, channels)
    down = wbuf[:, 1].reshape(hidden, channels)
    sub = 32
    shares = []
    parts = 2 if slab % 2 == 0 else 1
    span = points // parts
    lines = slab // parts
    for i in range(parts):
        begin, end = i * span, (i + 1) * span
        upper[begin:end, :] = dot(normed[begin:end, :], up, ((1,), (1,)))
        for t in range(begin, end, sub):
            u = upper[t : t + sub, :]
            th = jnp.tanh(SQRT_TWO_PI * (u + CUBIC * u * u * u))
            inner[t : t + sub, :] = th
            gated[t : t + sub, :] = (0.5 * u * (1.0 + th)).astype(BF16)
        mixed = dot(gated[begin:end, :], down, ((1,), (0,)))
        field = ext[HALF + i * lines : HALF + (i + 1) * lines].reshape(span, channels)
        residual = (field.astype(F32) + mixed).astype(BF16)
        resid[begin:end, :] = residual
        mine = dot(ro[...], residual, ((1,), (1,))).astype(BF16)
        looks[i, pl.ds(ens, 1)] = mine[None]
        for k in range(1, E):
            copy = remote(looks.at[i, ens], looks.at[i, ens], e_send.at[i, k], e_recv.at[i, ens],
                          at((ens + k) % E, lat))
            copy.start()
            shares.append(copy)
        mine = mine.astype(F32)
        for n in range(lines):
            outlook[:, i * lines + n, :] = mine[:, n * zonal : (n + 1) * zonal]

    look_o[0] = outlook[0:quantities].astype(BF16)

    for t in range(0, points, sub):
        u = upper[t : t + sub, :]
        th = inner[t : t + sub, :]
        inner[t : t + sub, :] = 0.5 * (1.0 + th) + 0.5 * u * (1.0 - th * th) * SQRT_TWO_PI * (
            1.0 + 3.0 * CUBIC * u * u
        )

    members = E
    pair_norm = 1.0 / (members * (members - 1))
    latitudes = slab * L
    row = lax.broadcasted_iota(jnp.int32, (slab, zonal), 0) + lat * slab
    area = jnp.cos(math.pi * ((row.astype(F32) + 0.5) / latitudes - 0.5))
    weights = area * (1.0 / (latitudes * zonal))
    truths[...] = jnp.zeros_like(truths)
    for i in range(slab):
        truths[0:quantities, i * zonal : (i + 1) * zonal] = obs[:, i, :]
    loss = jnp.zeros((1, span), F32)
    for i in range(parts):
        begin, end = i * span, (i + 1) * span
        weight = jnp.concatenate(
            [weights[i * lines + n : i * lines + n + 1] for n in range(lines)], axis=1)
        mine = looks[i, pl.ds(ens, 1)][0].astype(F32)
        miss = mine - truths[:, begin:end]
        square = miss * miss + SMOOTHING
        root = lax.rsqrt(square)
        miss_size = square * root
        miss_slope = miss * root
        spread = jnp.full((rows, span), math.sqrt(SMOOTHING), F32)
        ranks = jnp.zeros((rows, span), F32)
        for k in range(1, E):
            other = (ens + k) % E
            remote(looks.at[i, other], looks.at[i, other], e_send.at[i, k], e_recv.at[i, other],
                   at(other, lat)).wait_recv()
            gap = mine - looks[i, pl.ds(other, 1)][0].astype(F32)
            square = gap * gap + SMOOTHING
            root = lax.rsqrt(square)
            spread = spread + square * root
            ranks = ranks + gap * root
        truths[:, begin:end] = spread * (1.0 / (members - 1))
        part = weight * (miss_size / members - 0.5 * pair_norm * spread)
        loss = loss + jnp.sum(part[:quantities], axis=0, keepdims=True)
        flow = (weight * (miss_slope / members - pair_norm * ranks)).astype(BF16)
        flows[:, begin:end] = flow
        back_residual = dot(flow, ro[...], ((0,), (0,))).astype(BF16)
        back[begin:end, :] = back_residual
        upper[begin:end, :] = dot(back_residual, down, ((1,), (1,)))
        for t in range(begin, end, sub):
            gated_back[t : t + sub, :] = (
                upper[t : t + sub, :] * inner[t : t + sub, :]).astype(BF16)
    loss = jnp.sum(loss, axis=1, keepdims=True)

    def stash(slot, value):
        for l in range(L):
            for e in range(E):
                begin = (l * E + e) * piece
                grads[l % 2, e, l // 2, slot * piece : (slot + 1) * piece] = (
                    value[begin : begin + piece])

    def scatter(src, dst, send, recv, me, count, place):
        copies = [
            remote(src((me + k) % count), dst.at[me], send.at[k], recv.at[me],
                   place((me + k) % count))
            for k in range(1, count)
        ]
        for copy in copies:
            copy.start()
        return copies

    def arrive(dst, send, recv, me, count, place):
        for k in range(1, count):
            other = (me + k) % count
            remote(dst.at[other], dst.at[other], send.at[k], recv.at[other],
                   place(other)).wait_recv()

    def by_ens(e):
        return at(e, lat)

    def by_z(other):
        return at(ens, other * 2 + core)

    stash(0, dot(gated[...], back[...], ((0,), (0,))))
    stash(1, dot(gated_back[...], normed[...], ((0,), (0,))))
    halves = remote(grads.at[1 - core], rec_a, a_send.at[0], a_recv.at[0], at(ens, sibling))
    halves.start()

    out_grad = dot(flows[...], resid[...], ((1,), (0,)))
    chunk = SMALL_ROWS // (2 * E)

    def put(row, value):
        done = 0
        count = value.shape[0]
        while done < count:
            block, offset = divmod(row + done, chunk)
            take = min(count - done, chunk - offset)
            small[block, offset : offset + take, :] = value[done : done + take]
            done += take

    put(0, out_grad[:GRAD_ROW])

    upper[:, 0:channels] = dot(gated_back[...], up, ((1,), (0,)))
    gain_sum = jnp.zeros((1, channels), F32)
    for i in range(slab):
        back_norm = upper[i * zonal : (i + 1) * zonal, 0:channels]
        scaled = scaled_s[i]
        gain_sum = gain_sum + jnp.sum(back_norm * scaled, axis=0, keepdims=True)
        g = back_norm * gain[...]
        depth[i] = inv_s[i] * (
            g
            - jnp.mean(g, axis=-1, keepdims=True)
            - scaled * jnp.mean(g * scaled, axis=-1, keepdims=True)
        )
    halves.wait_recv()
    part_b[...] = grads[pl.ds(core, 1)][0] + rec_a[...]
    rec_b[pl.ds(ens, 1)] = part_b[pl.ds(ens, 1)]
    sent_b = scatter(lambda e: part_b.at[e], rec_b, b_send, b_recv, ens, E, by_ens)

    lane = 32

    def tap_columns(b, carry):
        sums = [jnp.zeros((8, channels), F32) for _ in range(SIDE)]
        for base in range(0, zonal, lane):
            g = [depth[i, base : base + lane, :] for i in range(slab)]
            wides = [jnp.zeros((lane, channels), F32)] * SIDE
            for r in range(2 * HALF + slab):
                x = wide[r, pl.ds(base + PAD - HALF + b, lane), :]
                for i in range(slab):
                    a = r - i
                    if 0 <= a < SIDE:
                        wides[a] = wides[a] + g[i] * x
            for a in range(SIDE):
                sums[a] = sums[a] + jnp.sum(wides[a].reshape(lane // 8, 8, channels), axis=0)
        for a in range(SIDE):
            tap_grad[pl.ds(a * SIDE + b, 1), :] = jnp.sum(sums[a], axis=0, keepdims=True)
        return carry

    lax.fori_loop(0, 4, tap_columns, 0)
    arrive(rec_b, b_send, b_recv, ens, E, by_ens)
    total = rec_b[0]
    for e in range(1, E):
        total = total + rec_b[e]
    part_c[...] = total
    rec_c[pl.ds(z, 1)] = part_c[pl.ds(z, 1)]
    sent_c = scatter(lambda o: part_c.at[o], rec_c, c_send, c_recv, z, Z, by_z)
    lax.fori_loop(4, SIDE, tap_columns, 0)
    put(GRAD_ROW, tap_grad[...])
    tail = GRAD_ROW + SIDE * SIDE
    put(tail, gain_sum)
    put(tail + 1, jnp.broadcast_to(loss, (1, channels)))
    put(tail + 2, jnp.zeros((SMALL_ROWS - tail - 2, channels), F32))

    plane = ens * 2 + core

    def by_plane(o):
        return at(o // 2, z * 2 + o % 2)

    small_b[pl.ds(plane, 1)] = small[pl.ds(plane, 1)]
    sent_p = scatter(lambda o: small.at[o], small_b, p_send, p_recv, plane, 2 * E, by_plane)
    arrive(rec_c, c_send, c_recv, z, Z, by_z)
    total = rec_c[0]
    for o in range(1, Z):
        total = total + rec_c[o]
    rec_d[pl.ds(ens, 1)] = total[None]
    sent_d = scatter(lambda e: rec_d.at[ens], rec_d, d_send, d_recv, ens, E, by_ens)
    arrive(small_b, p_send, p_recv, plane, 2 * E, by_plane)
    total = small_b[0]
    for o in range(1, 2 * E):
        total = total + small_b[o]
    small_pc[...] = total
    small_c[pl.ds(z, 1)] = total[None]
    sent_q = scatter(lambda o: small_pc, small_c, q_send, q_recv, z, Z, by_z)

    for i in range(slab):
        spread_o[0, :, i, :] = truths[0:quantities, i * zonal : (i + 1) * zonal]
    for copy in own + forwards + shares + [halves] + sent_b:
        copy.wait_send()

    @pl.when(lat < L - 1)
    def _():
        south.wait_send()

    @pl.when(lat > 0)
    def _():
        north.wait_send()

    arrive(small_c, q_send, q_recv, z, Z, by_z)
    total = small_c[0]
    for o in range(1, Z):
        total = total + small_c[o]
    small_d[pl.ds(plane, 1)] = total[None]
    sent_r = scatter(lambda o: small_d.at[plane], small_d, r_send, r_recv, plane, 2 * E, by_plane)
    arrive(rec_d, d_send, d_recv, ens, E, by_ens)
    for e in range(E):
        down_o[e * piece : (e + 1) * piece, :] = rec_d[e, 0:piece]
        up_o[e * piece : (e + 1) * piece, :] = rec_d[e, piece : 2 * piece]
    for copy in sent_c + sent_p + sent_d + sent_q:
        copy.wait_send()
    arrive(small_d, r_send, r_recv, plane, 2 * E, by_plane)
    final = jnp.concatenate([small_d[o] for o in range(2 * E)], axis=0)
    out_o[...] = final[:quantities]
    taps_o[...] = final[GRAD_ROW:tail]
    gain_o[...] = final[tail : tail + 1]
    crps_o[...] = final[tail + 1 : tail + 2, 0:1]

    for copy in sent_r:
        copy.wait_send()


def finish_kernel(*refs):
    count = (len(refs) - 1) // 2
    copies = [
        pltpu.make_async_copy(refs[n], refs[count + n], refs[-1].at[n]) for n in range(count)
    ]
    for copy in copies:
        copy.start()
    for copy in copies:
        copy.wait()


def on_device(
    features, random_perturbation, observed_truth, stencil_taps,
    affine_factor, widen_matrix, shrink_matrix, readout_matrix,
):
    E, L = lax.axis_size("ens"), lax.axis_size("lat")
    Z = L // 2
    _, slab, zonal, channels = random_perturbation.shape
    quantities = readout_matrix.shape[0]
    unit = widen_matrix.shape[0]
    hidden = unit * L
    piece = unit // E
    points = slab * zonal
    parts = 2 if slab % 2 == 0 else 1
    rows = -(-quantities // 16) * 16
    chunk = SMALL_ROWS // (2 * E)
    vmem = pl.BlockSpec(memory_space=pltpu.VMEM)
    dma = pltpu.SemaphoreType.DMA
    out = jax.ShapeDtypeStruct
    hbm = pl.BlockSpec(memory_space=pltpu.HBM)
    grid = (1, quantities, slab, zonal)
    shapes = [
        out((1, 1), F32),
        out((SIDE * SIDE, channels), F32),
        out((1, channels), F32),
        out((unit, channels), F32),
        out((unit, channels), F32),
        out((quantities, channels), F32),
        out(grid, BF16),
        out(grid, F32),
    ]
    results = pl.pallas_call(
        functools.partial(kernel, (E, L)),
        out_shape=shapes,
        in_specs=[hbm] * 8,
        out_specs=[vmem] * 8,
        scratch_shapes=[
            pltpu.VMEM((slab, zonal, channels), BF16),
            pltpu.VMEM((1, slab, zonal, channels), BF16),
            pltpu.VMEM((quantities, slab, zonal), F32),
            pltpu.VMEM((SIDE * SIDE, channels), F32),
            pltpu.VMEM((1, channels), F32),
            pltpu.VMEM((quantities, channels), BF16),
            pltpu.VMEM((slab + 2 * HALF, zonal, channels), BF16),
            pltpu.VMEM((slab + 2 * HALF, zonal + 2 * PAD, channels), F32),
            pltpu.VMEM((SIDE * SIDE, 8, channels), F32),
            pltpu.VMEM((slab, zonal, channels), F32),
            pltpu.VMEM((slab, zonal, channels), F32),
            pltpu.VMEM((slab, zonal, channels), F32),
            pltpu.VMEM((points, channels), BF16),
            pltpu.VMEM((points, hidden), F32),
            pltpu.VMEM((points, hidden), F32),
            pltpu.VMEM((points, hidden), BF16),
            pltpu.VMEM((rows, channels), BF16),
            pltpu.VMEM((parts, E, rows, points // parts), BF16),
            pltpu.VMEM((L, 2, unit, channels), BF16),
            pltpu.VMEM((points, channels), BF16),
            pltpu.VMEM((rows, points), BF16),
            pltpu.VMEM((points, channels), BF16),
            pltpu.VMEM((points, hidden), BF16),
            pltpu.VMEM((rows, slab, zonal), F32),
            pltpu.VMEM((rows, points), F32),
            pltpu.VMEM((SIDE * SIDE, channels), F32),
            pltpu.VMEM((2, E, Z, 2 * piece, channels), F32),
            pltpu.VMEM((E, Z, 2 * piece, channels), F32),
            pltpu.VMEM((E, Z, 2 * piece, channels), F32),
            pltpu.VMEM((E, Z, 2 * piece, channels), F32),
            pltpu.VMEM((Z, 2 * piece, channels), F32),
            pltpu.VMEM((Z, 2 * piece, channels), F32),
            pltpu.VMEM((E, 2 * piece, channels), F32),
            pltpu.VMEM((2 * E, chunk, channels), F32),
            pltpu.VMEM((2 * E, chunk, channels), F32),
            pltpu.VMEM((chunk, channels), F32),
            pltpu.VMEM((Z, chunk, channels), F32),
            pltpu.VMEM((2 * E, chunk, channels), F32),
            dma((8,)), dma((2,)), dma((2,)),
            dma((Z,)), dma((Z,)), dma((L,)),
            dma((slab, E)), dma((slab, E)),
            dma((1,)), dma((1,)),
            dma((E,)), dma((E,)),
            dma((Z,)), dma((Z,)),
            dma((E,)), dma((E,)),
            dma((2 * E,)), dma((2 * E,)),
            dma((Z,)), dma((Z,)),
            dma((2 * E,)), dma((2 * E,)),
        ],
        compiler_params=pltpu.CompilerParams(
            collective_id=0, has_side_effects=True, vmem_limit_bytes=40 * 1024 * 1024
        ),
        cost_estimate=pl.CostEstimate(
            flops=12 * points * channels * hidden, bytes_accessed=2_000_000, transcendentals=0
        ),
    )(
        *[
            pltpu.with_memory_space_constraint(value, pltpu.HBM)
            for value in (
                features, random_perturbation, observed_truth, stencil_taps,
                affine_factor.reshape(1, channels), widen_matrix, shrink_matrix, readout_matrix,
            )
        ]
    )
    crps, taps, gain, up, down, head, look, spread = pl.pallas_call(
        finish_kernel,
        out_shape=shapes,
        in_specs=[vmem] * 8,
        out_specs=[hbm] * 8,
        scratch_shapes=[dma((8,))],
        compiler_params=pltpu.CompilerParams(vmem_limit_bytes=8 * 1024 * 1024),
    )(*results)
    return (
        crps.reshape(()), taps, gain.reshape(channels), up, down, head, look, spread,
    )


def solution(mesh):
    in_specs = (
        P("lat", None, None),
        P("ens", "lat", None, None),
        P(None, "lat", None),
        P(),
        P(),
        P("lat", None),
        P("lat", None),
        P(),
    )
    out_specs = (
        P(),
        P(),
        P(),
        P("lat", None),
        P("lat", None),
        P(),
        P("ens", None, "lat", None),
        P("ens", None, "lat", None),
    )
    return jax.shard_map(
        on_device, mesh=mesh, in_specs=in_specs, out_specs=out_specs, check_vma=False
    )
```

```python
import functools
import math

import jax
import jax.numpy as jnp
from jax import lax
from jax.experimental import pallas as pl
from jax.experimental.pallas import tpu as pltpu
from jax.sharding import PartitionSpec as P

SIDE = 7
HALF = SIDE // 2
SQRT_TWO_PI = 0.7978845608028654
CUBIC = 0.044715
EPSILON = 1e-06
SMOOTHING = 0.01
PAD = 8
GRAD_ROW = 72
SMALL_ROWS = 128
F32 = jnp.float32
BF16 = jnp.bfloat16


def dot(a, b, dims):
    return lax.dot_general(a, b, (dims, ((), ())), preferred_element_type=F32)


def kernel(
    sizes,
    feat_h, noise_h, obs_h, taps_h, gain_h, widen_h, shrink_h, readout_h,
    crps_o, taps_o, gain_o, up_o, down_o, out_o, look_o, spread_o,
    feat, noise, obs, taps, gain, readout,
    ext, wide, tapb, depth, scaled_s, inv_s, normed, upper, inner, gated, ro, looks, wbuf,
    resid, flows, back, gated_back, outlook, truths, tap_grad,
    grads, rec_a, part_b, rec_b, part_c, rec_c, rec_d,
    small, small_b, small_pc, small_c, small_d,
    in_sem, halo_send, halo_recv, w_send, w_fwd, w_recv, e_send, e_recv,
    a_send, a_recv, b_send, b_recv, c_send, c_recv, d_send, d_recv,
    p_send, p_recv, q_send, q_recv, r_send, r_recv,
):
    E, L = sizes
    Z = L // 2
    slab, zonal, channels = feat.shape
    quantities = obs.shape[0]
    rows = ro.shape[0]
    points = slab * zonal
    hidden = L * wbuf.shape[2]
    piece = wbuf.shape[2] // E
    ens = lax.axis_index("ens")
    lat = lax.axis_index("lat")
    z = lat // 2
    core = lat % 2
    sibling = z * 2 + (1 - core)

    def at(e, l):
        return {"ens": e, "lat": l}

    def remote(src, dst, send, recv, where):
        return pltpu.make_async_remote_copy(
            src_ref=src, dst_ref=dst, send_sem=send, recv_sem=recv,
            device_id=where, device_id_type=pl.DeviceIdType.MESH,
        )

    barrier = pltpu.get_barrier_semaphore()
    for k in range(1, L):
        pl.semaphore_signal(barrier, inc=1, device_id=at(ens, (lat + k) % L),
                            device_id_type=pl.DeviceIdType.MESH)
    for k in range(1, E):
        for l in (lat, sibling):
            pl.semaphore_signal(barrier, inc=1, device_id=at((ens + k) % E, l),
                                device_id_type=pl.DeviceIdType.MESH)

    loads = [
        pltpu.make_async_copy(src, dst, in_sem.at[n])
        for n, (src, dst) in enumerate([
            (feat_h, feat), (noise_h, noise), (widen_h, wbuf.at[lat, 0]),
            (shrink_h, wbuf.at[lat, 1]), (taps_h, taps), (readout_h, readout),
            (gain_h, gain), (obs_h, obs),
        ])
    ]
    for copy in loads:
        copy.start()

    def widen_rows(start, count):
        block = ext[start : start + count].astype(F32)
        wide[start : start + count, PAD : PAD + zonal, :] = block
        wide[start : start + count, 0:PAD, :] = block[:, zonal - PAD :, :]
        wide[start : start + count, PAD + zonal :, :] = block[:, :PAD, :]

    loads[0].wait()
    loads[1].wait()
    field = (feat[...].astype(F32) + noise[0].astype(F32)).astype(BF16)
    ext[HALF : HALF + slab] = field
    pl.semaphore_wait(barrier, L - 1 + 2 * (E - 1))

    south = remote(ext.at[pl.ds(slab, HALF)], ext.at[pl.ds(0, HALF)],
                   halo_send.at[0], halo_recv.at[0], at(ens, jnp.minimum(lat + 1, L - 1)))
    north = remote(ext.at[pl.ds(HALF, HALF)], ext.at[pl.ds(HALF + slab, HALF)],
                   halo_send.at[1], halo_recv.at[1], at(ens, jnp.maximum(lat - 1, 0)))

    @pl.when(lat < L - 1)
    def _():
        south.start()

    @pl.when(lat > 0)
    def _():
        north.start()

    loads[2].wait()
    loads[3].wait()
    own = [
        remote(wbuf.at[lat], wbuf.at[lat], w_send.at[k], w_recv.at[lat],
               at(ens, ((z + k) % Z) * 2 + core))
        for k in range(1, Z)
    ]
    for copy in own:
        copy.start()
    forwards = [remote(wbuf.at[lat], wbuf.at[lat], w_fwd.at[0], w_recv.at[lat], at(ens, sibling))]
    forwards[0].start()

    widen_rows(HALF, slab)
    for copy in loads[4:]:
        copy.wait()
    for t in range(SIDE * SIDE):
        tapb[t] = jnp.broadcast_to(taps[t : t + 1, :], (8, channels))
    ro[...] = jnp.zeros_like(ro)
    ro[0:quantities, :] = readout[...]

    step = 32

    def convolve(ext_rows, fresh):
        def body(t, carry):
            base = pl.multiple_of(t * step, step)
            sums = []
            for i in range(slab):
                if fresh:
                    sums.append(jnp.zeros((step // 8, 8, channels), F32))
                else:
                    sums.append(depth[i, pl.ds(base, step), :].reshape(step // 8, 8, channels))
            for b in range(SIDE):
                for r in ext_rows:
                    x = wide[r, pl.ds(base + PAD - HALF + b, step), :].reshape(
                        step // 8, 8, channels)
                    for i in range(slab):
                        a = r - i
                        if 0 <= a < SIDE:
                            sums[i] = sums[i] + tapb[a * SIDE + b] * x
            for i in range(slab):
                depth[i, pl.ds(base, step), :] = sums[i].reshape(step, channels)
            return carry

        lax.fori_loop(0, zonal // step, body, 0)

    convolve(range(HALF, HALF + slab), True)

    for k in range(1, Z):
        other = ((z + k) % Z) * 2 + core
        remote(wbuf.at[other], wbuf.at[other], w_send.at[k], w_recv.at[other],
               at(ens, other)).wait_recv()
        copy = remote(wbuf.at[other], wbuf.at[other], w_fwd.at[k], w_recv.at[other],
                      at(ens, sibling))
        copy.start()
        forwards.append(copy)

    @pl.when(lat > 0)
    def _():
        south.wait_recv()
        widen_rows(0, HALF)

    @pl.when(lat == 0)
    def _():
        wide[0:HALF] = jnp.zeros((HALF, zonal + 2 * PAD, channels), F32)

    @pl.when(lat < L - 1)
    def _():
        north.wait_recv()
        widen_rows(HALF + slab, HALF)

    @pl.when(lat == L - 1)
    def _():
        wide[HALF + slab :] = jnp.zeros((HALF, zonal + 2 * PAD, channels), F32)

    convolve([*range(HALF), *range(HALF + slab, 2 * HALF + slab)], False)

    for i in range(slab):
        d = depth[i]
        centred = d - jnp.mean(d, axis=-1, keepdims=True)
        inverse = lax.rsqrt(jnp.mean(centred * centred, axis=-1, keepdims=True) + EPSILON)
        scaled = centred * inverse
        scaled_s[i] = scaled
        inv_s[i] = jnp.broadcast_to(inverse, (zonal, channels))
        normed[i * zonal : (i + 1) * zonal, :] = (gain[...] * scaled).astype(BF16)

    for k in range(Z):
        other = ((z + k) % Z) * 2 + (1 - core)
        remote(wbuf.at[other], wbuf.at[other], w_fwd.at[k], w_recv.at[other],
               at(ens, sibling)).wait_recv()

    up = wbuf[:, 0].reshape(hidden, channels)
    down = wbuf[:, 1].reshape(hidden, channels)
    sub = 32
    shares = []
    parts = slab
    span = points // parts
    lines = slab // parts
    for i in range(parts):
        begin, end = i * span, (i + 1) * span
        upper[begin:end, :] = dot(normed[begin:end, :], up, ((1,), (1,)))
        for t in range(begin, end, sub):
            u = upper[t : t + sub, :]
            th = jnp.tanh(SQRT_TWO_PI * (u + CUBIC * u * u * u))
            inner[t : t + sub, :] = th
            gated[t : t + sub, :] = (0.5 * u * (1.0 + th)).astype(BF16)
        mixed = dot(gated[begin:end, :], down, ((1,), (0,)))
        field = ext[HALF + i * lines : HALF + (i + 1) * lines].reshape(span, channels)
        residual = (field.astype(F32) + mixed).astype(BF16)
        resid[begin:end, :] = residual
        mine = dot(ro[...], residual, ((1,), (1,))).astype(BF16)
        looks[i, pl.ds(ens, 1)] = mine[None]
        for k in range(1, E):
            copy = remote(looks.at[i, ens], looks.at[i, ens], e_send.at[i, k], e_recv.at[i, ens],
                          at((ens + k) % E, lat))
            copy.start()
            shares.append(copy)
        mine = mine.astype(F32)
        for n in range(lines):
            outlook[:, i * lines + n, :] = mine[:, n * zonal : (n + 1) * zonal]

    look_o[0] = outlook[0:quantities].astype(BF16)

    for t in range(0, points, sub):
        u = upper[t : t + sub, :]
        th = inner[t : t + sub, :]
        inner[t : t + sub, :] = 0.5 * (1.0 + th) + 0.5 * u * (1.0 - th * th) * SQRT_TWO_PI * (
            1.0 + 3.0 * CUBIC * u * u
        )

    members = E
    pair_norm = 1.0 / (members * (members - 1))
    latitudes = slab * L
    row = lax.broadcasted_iota(jnp.int32, (slab, zonal), 0) + lat * slab
    area = jnp.cos(math.pi * ((row.astype(F32) + 0.5) / latitudes - 0.5))
    weights = area * (1.0 / (latitudes * zonal))
    truths[...] = jnp.zeros_like(truths)
    for i in range(slab):
        truths[0:quantities, i * zonal : (i + 1) * zonal] = obs[:, i, :]
    loss = jnp.zeros((1, span), F32)
    for i in range(parts):
        begin, end = i * span, (i + 1) * span
        weight = jnp.concatenate(
            [weights[i * lines + n : i * lines + n + 1] for n in range(lines)], axis=1)
        mine = looks[i, pl.ds(ens, 1)][0].astype(F32)
        miss = mine - truths[:, begin:end]
        square = miss * miss + SMOOTHING
        root = lax.rsqrt(square)
        miss_size = square * root
        miss_slope = miss * root
        spread = jnp.full((rows, span), math.sqrt(SMOOTHING), F32)
        ranks = jnp.zeros((rows, span), F32)
        for k in range(1, E):
            other = (ens + k) % E
            remote(looks.at[i, other], looks.at[i, other], e_send.at[i, k], e_recv.at[i, other],
                   at(other, lat)).wait_recv()
            gap = mine - looks[i, pl.ds(other, 1)][0].astype(F32)
            square = gap * gap + SMOOTHING
            root = lax.rsqrt(square)
            spread = spread + square * root
            ranks = ranks + gap * root
        truths[:, begin:end] = spread * (1.0 / (members - 1))
        part = weight * (miss_size / members - 0.5 * pair_norm * spread)
        loss = loss + jnp.sum(part[:quantities], axis=0, keepdims=True)
        flow = (weight * (miss_slope / members - pair_norm * ranks)).astype(BF16)
        flows[:, begin:end] = flow
        back_residual = dot(flow, ro[...], ((0,), (0,))).astype(BF16)
        back[begin:end, :] = back_residual
        upper[begin:end, :] = dot(back_residual, down, ((1,), (1,)))
        for t in range(begin, end, sub):
            gated_back[t : t + sub, :] = (
                upper[t : t + sub, :] * inner[t : t + sub, :]).astype(BF16)
    loss = jnp.sum(loss, axis=1, keepdims=True)

    def stash(slot, value):
        for l in range(L):
            for e in range(E):
                begin = (l * E + e) * piece
                grads[l % 2, e, l // 2, slot * piece : (slot + 1) * piece] = (
                    value[begin : begin + piece])

    def scatter(src, dst, send, recv, me, count, place):
        copies = [
            remote(src((me + k) % count), dst.at[me], send.at[k], recv.at[me],
                   place((me + k) % count))
            for k in range(1, count)
        ]
        for copy in copies:
            copy.start()
        return copies

    def arrive(dst, send, recv, me, count, place):
        for k in range(1, count):
            other = (me + k) % count
            remote(dst.at[other], dst.at[other], send.at[k], recv.at[other],
                   place(other)).wait_recv()

    def by_ens(e):
        return at(e, lat)

    def by_z(other):
        return at(ens, other * 2 + core)

    stash(0, dot(gated[...], back[...], ((0,), (0,))))
    stash(1, dot(gated_back[...], normed[...], ((0,), (0,))))
    halves = remote(grads.at[1 - core], rec_a, a_send.at[0], a_recv.at[0], at(ens, sibling))
    halves.start()

    out_grad = dot(flows[...], resid[...], ((1,), (0,)))
    chunk = SMALL_ROWS // (2 * E)

    def put(row, value):
        done = 0
        count = value.shape[0]
        while done < count:
            block, offset = divmod(row + done, chunk)
            take = min(count - done, chunk - offset)
            small[block, offset : offset + take, :] = value[done : done + take]
            done += take

    put(0, out_grad[:GRAD_ROW])

    upper[:, 0:channels] = dot(gated_back[...], up, ((1,), (0,)))
    gain_sum = jnp.zeros((1, channels), F32)
    for i in range(slab):
        back_norm = upper[i * zonal : (i + 1) * zonal, 0:channels]
        scaled = scaled_s[i]
        gain_sum = gain_sum + jnp.sum(back_norm * scaled, axis=0, keepdims=True)
        g = back_norm * gain[...]
        depth[i] = inv_s[i] * (
            g
            - jnp.mean(g, axis=-1, keepdims=True)
            - scaled * jnp.mean(g * scaled, axis=-1, keepdims=True)
        )
    halves.wait_recv()
    part_b[...] = grads[pl.ds(core, 1)][0] + rec_a[...]
    rec_b[pl.ds(ens, 1)] = part_b[pl.ds(ens, 1)]
    sent_b = scatter(lambda e: part_b.at[e], rec_b, b_send, b_recv, ens, E, by_ens)

    lane = 32

    def tap_columns(b, carry):
        sums = [jnp.zeros((8, channels), F32) for _ in range(SIDE)]
        for base in range(0, zonal, lane):
            g = [depth[i, base : base + lane, :] for i in range(slab)]
            wides = [jnp.zeros((lane, channels), F32)] * SIDE
            for r in range(2 * HALF + slab):
                x = wide[r, pl.ds(base + PAD - HALF + b, lane), :]
                for i in range(slab):
                    a = r - i
                    if 0 <= a < SIDE:
                        wides[a] = wides[a] + g[i] * x
            for a in range(SIDE):
                sums[a] = sums[a] + jnp.sum(wides[a].reshape(lane // 8, 8, channels), axis=0)
        for a in range(SIDE):
            tap_grad[pl.ds(a * SIDE + b, 1), :] = jnp.sum(sums[a], axis=0, keepdims=True)
        return carry

    lax.fori_loop(0, SIDE, tap_columns, 0)
    put(GRAD_ROW, tap_grad[...])
    tail = GRAD_ROW + SIDE * SIDE
    put(tail, gain_sum)
    put(tail + 1, jnp.broadcast_to(loss, (1, channels)))
    put(tail + 2, jnp.zeros((SMALL_ROWS - tail - 2, channels), F32))

    plane = ens * 2 + core

    def by_plane(o):
        return at(o // 2, z * 2 + o % 2)

    small_b[pl.ds(plane, 1)] = small[pl.ds(plane, 1)]
    sent_p = scatter(lambda o: small.at[o], small_b, p_send, p_recv, plane, 2 * E, by_plane)
    arrive(rec_b, b_send, b_recv, ens, E, by_ens)
    total = rec_b[0]
    for e in range(1, E):
        total = total + rec_b[e]
    part_c[...] = total
    rec_c[pl.ds(z, 1)] = part_c[pl.ds(z, 1)]
    sent_c = scatter(lambda o: part_c.at[o], rec_c, c_send, c_recv, z, Z, by_z)
    arrive(small_b, p_send, p_recv, plane, 2 * E, by_plane)
    total = small_b[0]
    for o in range(1, 2 * E):
        total = total + small_b[o]
    small_pc[...] = total
    small_c[pl.ds(z, 1)] = total[None]
    sent_q = scatter(lambda o: small_pc, small_c, q_send, q_recv, z, Z, by_z)

    for i in range(slab):
        spread_o[0, :, i, :] = truths[0:quantities, i * zonal : (i + 1) * zonal]
    for copy in own + forwards + shares + [halves] + sent_b:
        copy.wait_send()

    @pl.when(lat < L - 1)
    def _():
        south.wait_send()

    @pl.when(lat > 0)
    def _():
        north.wait_send()

    arrive(rec_c, c_send, c_recv, z, Z, by_z)
    total = rec_c[0]
    for o in range(1, Z):
        total = total + rec_c[o]
    rec_d[pl.ds(ens, 1)] = total[None]
    sent_d = scatter(lambda e: rec_d.at[ens], rec_d, d_send, d_recv, ens, E, by_ens)
    arrive(small_c, q_send, q_recv, z, Z, by_z)
    total = small_c[0]
    for o in range(1, Z):
        total = total + small_c[o]
    small_d[pl.ds(plane, 1)] = total[None]
    sent_r = scatter(lambda o: small_d.at[plane], small_d, r_send, r_recv, plane, 2 * E, by_plane)
    arrive(rec_d, d_send, d_recv, ens, E, by_ens)
    for e in range(E):
        down_o[e * piece : (e + 1) * piece, :] = rec_d[e, 0:piece]
        up_o[e * piece : (e + 1) * piece, :] = rec_d[e, piece : 2 * piece]
    for copy in sent_c + sent_p + sent_d + sent_q:
        copy.wait_send()
    arrive(small_d, r_send, r_recv, plane, 2 * E, by_plane)
    final = jnp.concatenate([small_d[o] for o in range(2 * E)], axis=0)
    out_o[...] = final[:quantities]
    taps_o[...] = final[GRAD_ROW:tail]
    gain_o[...] = final[tail : tail + 1]
    crps_o[...] = final[tail + 1 : tail + 2, 0:1]

    for copy in sent_r:
        copy.wait_send()


def finish_kernel(*refs):
    count = (len(refs) - 1) // 2
    copies = [
        pltpu.make_async_copy(refs[n], refs[count + n], refs[-1].at[n]) for n in range(count)
    ]
    for copy in copies:
        copy.start()
    for copy in copies:
        copy.wait()


def on_device(
    features, random_perturbation, observed_truth, stencil_taps,
    affine_factor, widen_matrix, shrink_matrix, readout_matrix,
):
    E, L = lax.axis_size("ens"), lax.axis_size("lat")
    Z = L // 2
    _, slab, zonal, channels = random_perturbation.shape
    quantities = readout_matrix.shape[0]
    unit = widen_matrix.shape[0]
    hidden = unit * L
    piece = unit // E
    points = slab * zonal
    parts = slab
    rows = -(-quantities // 16) * 16
    chunk = SMALL_ROWS // (2 * E)
    vmem = pl.BlockSpec(memory_space=pltpu.VMEM)
    dma = pltpu.SemaphoreType.DMA
    out = jax.ShapeDtypeStruct
    hbm = pl.BlockSpec(memory_space=pltpu.HBM)
    grid = (1, quantities, slab, zonal)
    shapes = [
        out((1, 1), F32),
        out((SIDE * SIDE, channels), F32),
        out((1, channels), F32),
        out((unit, channels), F32),
        out((unit, channels), F32),
        out((quantities, channels), F32),
        out(grid, BF16),
        out(grid, F32),
    ]
    results = pl.pallas_call(
        functools.partial(kernel, (E, L)),
        out_shape=shapes,
        in_specs=[hbm] * 8,
        out_specs=[vmem] * 8,
        scratch_shapes=[
            pltpu.VMEM((slab, zonal, channels), BF16),
            pltpu.VMEM((1, slab, zonal, channels), BF16),
            pltpu.VMEM((quantities, slab, zonal), F32),
            pltpu.VMEM((SIDE * SIDE, channels), F32),
            pltpu.VMEM((1, channels), F32),
            pltpu.VMEM((quantities, channels), BF16),
            pltpu.VMEM((slab + 2 * HALF, zonal, channels), BF16),
            pltpu.VMEM((slab + 2 * HALF, zonal + 2 * PAD, channels), F32),
            pltpu.VMEM((SIDE * SIDE, 8, channels), F32),
            pltpu.VMEM((slab, zonal, channels), F32),
            pltpu.VMEM((slab, zonal, channels), F32),
            pltpu.VMEM((slab, zonal, channels), F32),
            pltpu.VMEM((points, channels), BF16),
            pltpu.VMEM((points, hidden), F32),
            pltpu.VMEM((points, hidden), F32),
            pltpu.VMEM((points, hidden), BF16),
            pltpu.VMEM((rows, channels), BF16),
            pltpu.VMEM((parts, E, rows, points // parts), BF16),
            pltpu.VMEM((L, 2, unit, channels), BF16),
            pltpu.VMEM((points, channels), BF16),
            pltpu.VMEM((rows, points), BF16),
            pltpu.VMEM((points, channels), BF16),
            pltpu.VMEM((points, hidden), BF16),
            pltpu.VMEM((rows, slab, zonal), F32),
            pltpu.VMEM((rows, points), F32),
            pltpu.VMEM((SIDE * SIDE, channels), F32),
            pltpu.VMEM((2, E, Z, 2 * piece, channels), F32),
            pltpu.VMEM((E, Z, 2 * piece, channels), F32),
            pltpu.VMEM((E, Z, 2 * piece, channels), F32),
            pltpu.VMEM((E, Z, 2 * piece, channels), F32),
            pltpu.VMEM((Z, 2 * piece, channels), F32),
            pltpu.VMEM((Z, 2 * piece, channels), F32),
            pltpu.VMEM((E, 2 * piece, channels), F32),
            pltpu.VMEM((2 * E, chunk, channels), F32),
            pltpu.VMEM((2 * E, chunk, channels), F32),
            pltpu.VMEM((chunk, channels), F32),
            pltpu.VMEM((Z, chunk, channels), F32),
            pltpu.VMEM((2 * E, chunk, channels), F32),
            dma((8,)), dma((2,)), dma((2,)),
            dma((Z,)), dma((Z,)), dma((L,)),
            dma((slab, E)), dma((slab, E)),
            dma((1,)), dma((1,)),
            dma((E,)), dma((E,)),
            dma((Z,)), dma((Z,)),
            dma((E,)), dma((E,)),
            dma((2 * E,)), dma((2 * E,)),
            dma((Z,)), dma((Z,)),
            dma((2 * E,)), dma((2 * E,)),
        ],
        compiler_params=pltpu.CompilerParams(
            collective_id=0, has_side_effects=True, vmem_limit_bytes=40 * 1024 * 1024
        ),
        cost_estimate=pl.CostEstimate(
            flops=12 * points * channels * hidden, bytes_accessed=2_000_000, transcendentals=0
        ),
    )(
        *[
            pltpu.with_memory_space_constraint(value, pltpu.HBM)
            for value in (
                features, random_perturbation, observed_truth, stencil_taps,
                affine_factor.reshape(1, channels), widen_matrix, shrink_matrix, readout_matrix,
            )
        ]
    )
    crps, taps, gain, up, down, head, look, spread = pl.pallas_call(
        finish_kernel,
        out_shape=shapes,
        in_specs=[vmem] * 8,
        out_specs=[hbm] * 8,
        scratch_shapes=[dma((8,))],
        compiler_params=pltpu.CompilerParams(vmem_limit_bytes=8 * 1024 * 1024),
    )(*results)
    return (
        crps.reshape(()), taps, gain.reshape(channels), up, down, head, look, spread,
    )


def solution(mesh):
    in_specs = (
        P("lat", None, None),
        P("ens", "lat", None, None),
        P(None, "lat", None),
        P(),
        P(),
        P("lat", None),
        P("lat", None),
        P(),
    )
    out_specs = (
        P(),
        P(),
        P(),
        P("lat", None),
        P("lat", None),
        P(),
        P("ens", None, "lat", None),
        P("ens", None, "lat", None),
    )
    return jax.shard_map(
        on_device, mesh=mesh, in_specs=in_specs, out_specs=out_specs, check_vma=False
    )
```

```python
import functools
import math

import jax
import jax.numpy as jnp
from jax import lax
from jax.experimental import pallas as pl
from jax.experimental.pallas import tpu as pltpu
from jax.sharding import PartitionSpec as P

SIDE = 7
HALF = SIDE // 2
SQRT_TWO_PI = 0.7978845608028654
CUBIC = 0.044715
EPSILON = 1e-06
SMOOTHING = 0.01
PAD = 8
GRAD_ROW = 72
SMALL_ROWS = 128
F32 = jnp.float32
BF16 = jnp.bfloat16


def dot(a, b, dims):
    return lax.dot_general(a, b, (dims, ((), ())), preferred_element_type=F32)


def kernel(
    sizes,
    feat_h, noise_h, obs_h, taps_h, gain_h, widen_h, shrink_h, readout_h,
    crps_o, taps_o, gain_o, up_o, down_o, out_o, look_o, spread_o,
    feat, noise, obs, taps, gain, readout,
    ext, wide, tapb, depth, scaled_s, inv_s, normed, upper, inner, gated, ro, looks, wbuf,
    resid, flows, back, gated_back, outlook, truths, tap_grad,
    grads, rec_a, part_b, rec_b, part_c, rec_c, rec_d,
    small, small_b, small_pc, small_c, small_d,
    in_sem, halo_send, halo_recv, w_send, w_fwd, w_recv, e_send, e_recv,
    a_send, a_recv, b_send, b_recv, c_send, c_recv, d_send, d_recv,
    p_send, p_recv, q_send, q_recv, r_send, r_recv,
):
    E, L = sizes
    Z = L // 2
    slab, zonal, channels = feat.shape
    quantities = obs.shape[0]
    rows = ro.shape[0]
    points = slab * zonal
    hidden = L * wbuf.shape[2]
    piece = wbuf.shape[2] // E
    ens = lax.axis_index("ens")
    lat = lax.axis_index("lat")
    z = lat // 2
    core = lat % 2
    sibling = z * 2 + (1 - core)

    def at(e, l):
        return {"ens": e, "lat": l}

    def remote(src, dst, send, recv, where):
        return pltpu.make_async_remote_copy(
            src_ref=src, dst_ref=dst, send_sem=send, recv_sem=recv,
            device_id=where, device_id_type=pl.DeviceIdType.MESH,
        )

    barrier = pltpu.get_barrier_semaphore()
    for k in range(1, L):
        pl.semaphore_signal(barrier, inc=1, device_id=at(ens, (lat + k) % L),
                            device_id_type=pl.DeviceIdType.MESH)
    for k in range(1, E):
        for l in (lat, sibling):
            pl.semaphore_signal(barrier, inc=1, device_id=at((ens + k) % E, l),
                                device_id_type=pl.DeviceIdType.MESH)

    loads = [
        pltpu.make_async_copy(src, dst, in_sem.at[n])
        for n, (src, dst) in enumerate([
            (feat_h, feat), (noise_h, noise), (widen_h, wbuf.at[lat, 0]),
            (shrink_h, wbuf.at[lat, 1]), (taps_h, taps), (readout_h, readout),
            (gain_h, gain), (obs_h, obs),
        ])
    ]
    for copy in loads:
        copy.start()

    def widen_rows(start, count):
        block = ext[start : start + count].astype(F32)
        wide[start : start + count, PAD : PAD + zonal, :] = block
        wide[start : start + count, 0:PAD, :] = block[:, zonal - PAD :, :]
        wide[start : start + count, PAD + zonal :, :] = block[:, :PAD, :]

    loads[0].wait()
    loads[1].wait()
    field = (feat[...].astype(F32) + noise[0].astype(F32)).astype(BF16)
    ext[HALF : HALF + slab] = field
    pl.semaphore_wait(barrier, L - 1 + 2 * (E - 1))

    south = remote(ext.at[pl.ds(slab, HALF)], ext.at[pl.ds(0, HALF)],
                   halo_send.at[0], halo_recv.at[0], at(ens, jnp.minimum(lat + 1, L - 1)))
    north = remote(ext.at[pl.ds(HALF, HALF)], ext.at[pl.ds(HALF + slab, HALF)],
                   halo_send.at[1], halo_recv.at[1], at(ens, jnp.maximum(lat - 1, 0)))

    @pl.when(lat < L - 1)
    def _():
        south.start()

    @pl.when(lat > 0)
    def _():
        north.start()

    loads[2].wait()
    loads[3].wait()
    own = [
        remote(wbuf.at[lat], wbuf.at[lat], w_send.at[k], w_recv.at[lat],
               at(ens, ((z + k) % Z) * 2 + core))
        for k in range(1, Z)
    ]
    for copy in own:
        copy.start()
    forwards = [remote(wbuf.at[lat], wbuf.at[lat], w_fwd.at[0], w_recv.at[lat], at(ens, sibling))]
    forwards[0].start()

    widen_rows(HALF, slab)
    for copy in loads[4:]:
        copy.wait()
    for t in range(SIDE * SIDE):
        tapb[t] = jnp.broadcast_to(taps[t : t + 1, :], (8, channels))
    ro[...] = jnp.zeros_like(ro)
    ro[0:quantities, :] = readout[...]

    step = 32

    def convolve(ext_rows, fresh):
        def body(t, carry):
            base = pl.multiple_of(t * step, step)
            sums = []
            for i in range(slab):
                if fresh:
                    sums.append(jnp.zeros((step // 8, 8, channels), F32))
                else:
                    sums.append(depth[i, pl.ds(base, step), :].reshape(step // 8, 8, channels))
            for b in range(SIDE):
                for r in ext_rows:
                    x = wide[r, pl.ds(base + PAD - HALF + b, step), :].reshape(
                        step // 8, 8, channels)
                    for i in range(slab):
                        a = r - i
                        if 0 <= a < SIDE:
                            sums[i] = sums[i] + tapb[a * SIDE + b] * x
            for i in range(slab):
                depth[i, pl.ds(base, step), :] = sums[i].reshape(step, channels)
            return carry

        lax.fori_loop(0, zonal // step, body, 0)

    convolve(range(HALF, HALF + slab), True)

    latitudes = slab * L
    row = lax.broadcasted_iota(jnp.int32, (slab, zonal), 0) + lat * slab
    area = jnp.cos(math.pi * ((row.astype(F32) + 0.5) / latitudes - 0.5))
    weights = area * (1.0 / (latitudes * zonal))
    truths[...] = jnp.zeros_like(truths)
    for i in range(slab):
        truths[0:quantities, i * zonal : (i + 1) * zonal] = obs[:, i, :]

    for k in range(1, Z):
        other = ((z + k) % Z) * 2 + core
        remote(wbuf.at[other], wbuf.at[other], w_send.at[k], w_recv.at[other],
               at(ens, other)).wait_recv()
        copy = remote(wbuf.at[other], wbuf.at[other], w_fwd.at[k], w_recv.at[other],
                      at(ens, sibling))
        copy.start()
        forwards.append(copy)

    @pl.when(lat > 0)
    def _():
        south.wait_recv()
        widen_rows(0, HALF)

    @pl.when(lat == 0)
    def _():
        wide[0:HALF] = jnp.zeros((HALF, zonal + 2 * PAD, channels), F32)

    @pl.when(lat < L - 1)
    def _():
        north.wait_recv()
        widen_rows(HALF + slab, HALF)

    @pl.when(lat == L - 1)
    def _():
        wide[HALF + slab :] = jnp.zeros((HALF, zonal + 2 * PAD, channels), F32)

    convolve([*range(HALF), *range(HALF + slab, 2 * HALF + slab)], False)

    for i in range(slab):
        d = depth[i]
        centred = d - jnp.mean(d, axis=-1, keepdims=True)
        inverse = lax.rsqrt(jnp.mean(centred * centred, axis=-1, keepdims=True) + EPSILON)
        scaled = centred * inverse
        scaled_s[i] = scaled
        inv_s[i] = jnp.broadcast_to(inverse, (zonal, channels))
        normed[i * zonal : (i + 1) * zonal, :] = (gain[...] * scaled).astype(BF16)

    for k in range(Z):
        other = ((z + k) % Z) * 2 + (1 - core)
        remote(wbuf.at[other], wbuf.at[other], w_fwd.at[k], w_recv.at[other],
               at(ens, sibling)).wait_recv()

    up = wbuf[:, 0].reshape(hidden, channels)
    down = wbuf[:, 1].reshape(hidden, channels)
    sub = 32
    shares = []
    parts = slab
    span = points // parts
    lines = slab // parts
    def activate(i):
        for t in range(i * span, (i + 1) * span, sub):
            u = upper[t : t + sub, :]
            th = jnp.tanh(SQRT_TWO_PI * (u + CUBIC * u * u * u))
            inner[t : t + sub, :] = th
            gated[t : t + sub, :] = (0.5 * u * (1.0 + th)).astype(BF16)

    upper[...] = dot(normed[...], up, ((1,), (1,)))
    activate(0)
    for i in range(parts):
        begin, end = i * span, (i + 1) * span
        if i + 1 < parts:
            activate(i + 1)
        mixed = dot(gated[begin:end, :], down, ((1,), (0,)))
        field = ext[HALF + i * lines : HALF + (i + 1) * lines].reshape(span, channels)
        residual = (field.astype(F32) + mixed).astype(BF16)
        resid[begin:end, :] = residual
        mine = dot(ro[...], residual, ((1,), (1,))).astype(BF16)
        looks[i, pl.ds(ens, 1)] = mine[None]
        for k in range(1, E):
            copy = remote(looks.at[i, ens], looks.at[i, ens], e_send.at[i, k], e_recv.at[i, ens],
                          at((ens + k) % E, lat))
            copy.start()
            shares.append(copy)


    for t in range(0, points, sub):
        u = upper[t : t + sub, :]
        th = inner[t : t + sub, :]
        inner[t : t + sub, :] = 0.5 * (1.0 + th) + 0.5 * u * (1.0 - th * th) * SQRT_TWO_PI * (
            1.0 + 3.0 * CUBIC * u * u
        )

    members = E
    pair_norm = 1.0 / (members * (members - 1))
    def descend(i):
        begin, end = i * span, (i + 1) * span
        back_residual = dot(flows[:, begin:end], ro[...], ((0,), (0,))).astype(BF16)
        back[begin:end, :] = back_residual
        upper[begin:end, :] = dot(back_residual, down, ((1,), (1,)))
        for t in range(begin, end, sub):
            gated_back[t : t + sub, :] = (
                upper[t : t + sub, :] * inner[t : t + sub, :]).astype(BF16)

    loss = jnp.zeros((1, span), F32)
    for i in range(parts):
        begin, end = i * span, (i + 1) * span
        weight = jnp.concatenate(
            [weights[i * lines + n : i * lines + n + 1] for n in range(lines)], axis=1)
        mine = looks[i, pl.ds(ens, 1)][0].astype(F32)
        miss = mine - truths[:, begin:end]
        square = miss * miss + SMOOTHING
        root = lax.rsqrt(square)
        miss_size = square * root
        miss_slope = miss * root
        spread = jnp.full((rows, span), math.sqrt(SMOOTHING), F32)
        ranks = jnp.zeros((rows, span), F32)
        for k in range(1, E):
            other = (ens + k) % E
            remote(looks.at[i, other], looks.at[i, other], e_send.at[i, k], e_recv.at[i, other],
                   at(other, lat)).wait_recv()
            gap = mine - looks[i, pl.ds(other, 1)][0].astype(F32)
            square = gap * gap + SMOOTHING
            root = lax.rsqrt(square)
            spread = spread + square * root
            ranks = ranks + gap * root
        truths[:, begin:end] = spread * (1.0 / (members - 1))
        part = weight * (miss_size / members - 0.5 * pair_norm * spread)
        loss = loss + jnp.sum(part[:quantities], axis=0, keepdims=True)
        flow = (weight * (miss_slope / members - pair_norm * ranks)).astype(BF16)
        flows[:, begin:end] = flow
        if i > 0:
            descend(i - 1)
    descend(parts - 1)
    loss = jnp.sum(loss, axis=1, keepdims=True)

    def stash(slot, value):
        for l in range(L):
            for e in range(E):
                begin = (l * E + e) * piece
                grads[l % 2, e, l // 2, slot * piece : (slot + 1) * piece] = (
                    value[begin : begin + piece])

    def scatter(src, dst, send, recv, me, count, place):
        copies = [
            remote(src((me + k) % count), dst.at[me], send.at[k], recv.at[me],
                   place((me + k) % count))
            for k in range(1, count)
        ]
        for copy in copies:
            copy.start()
        return copies

    def arrive(dst, send, recv, me, count, place):
        for k in range(1, count):
            other = (me + k) % count
            remote(dst.at[other], dst.at[other], send.at[k], recv.at[other],
                   place(other)).wait_recv()

    def by_ens(e):
        return at(e, lat)

    def by_z(other):
        return at(ens, other * 2 + core)

    stash(0, dot(gated[...], back[...], ((0,), (0,))))
    stash(1, dot(gated_back[...], normed[...], ((0,), (0,))))
    halves = remote(grads.at[1 - core], rec_a, a_send.at[0], a_recv.at[0], at(ens, sibling))
    halves.start()

    out_grad = dot(flows[...], resid[...], ((1,), (0,)))
    chunk = SMALL_ROWS // (2 * E)

    def put(row, value):
        done = 0
        count = value.shape[0]
        while done < count:
            block, offset = divmod(row + done, chunk)
            take = min(count - done, chunk - offset)
            small[block, offset : offset + take, :] = value[done : done + take]
            done += take

    put(0, out_grad[:GRAD_ROW])

    upper[:, 0:channels] = dot(gated_back[...], up, ((1,), (0,)))
    gain_sum = jnp.zeros((1, channels), F32)
    for i in range(slab):
        if i == slab // 2:
            halves.wait_recv()
            part_b[...] = grads[pl.ds(core, 1)][0] + rec_a[...]
            rec_b[pl.ds(ens, 1)] = part_b[pl.ds(ens, 1)]
            sent_b = scatter(lambda e: part_b.at[e], rec_b, b_send, b_recv, ens, E, by_ens)
        back_norm = upper[i * zonal : (i + 1) * zonal, 0:channels]
        scaled = scaled_s[i]
        gain_sum = gain_sum + jnp.sum(back_norm * scaled, axis=0, keepdims=True)
        g = back_norm * gain[...]
        depth[i] = inv_s[i] * (
            g
            - jnp.mean(g, axis=-1, keepdims=True)
            - scaled * jnp.mean(g * scaled, axis=-1, keepdims=True)
        )
    lane = 32

    def tap_columns(b, carry):
        sums = [jnp.zeros((8, channels), F32) for _ in range(SIDE)]
        for base in range(0, zonal, lane):
            g = [depth[i, base : base + lane, :] for i in range(slab)]
            wides = [jnp.zeros((lane, channels), F32)] * SIDE
            for r in range(2 * HALF + slab):
                x = wide[r, pl.ds(base + PAD - HALF + b, lane), :]
                for i in range(slab):
                    a = r - i
                    if 0 <= a < SIDE:
                        wides[a] = wides[a] + g[i] * x
            for a in range(SIDE):
                sums[a] = sums[a] + jnp.sum(wides[a].reshape(lane // 8, 8, channels), axis=0)
        for a in range(SIDE):
            tap_grad[pl.ds(a * SIDE + b, 1), :] = jnp.sum(sums[a], axis=0, keepdims=True)
        return carry

    lax.fori_loop(0, SIDE, tap_columns, 0)
    put(GRAD_ROW, tap_grad[...])
    tail = GRAD_ROW + SIDE * SIDE
    put(tail, gain_sum)
    put(tail + 1, jnp.broadcast_to(loss, (1, channels)))
    put(tail + 2, jnp.zeros((SMALL_ROWS - tail - 2, channels), F32))

    plane = ens * 2 + core

    def by_plane(o):
        return at(o // 2, z * 2 + o % 2)

    small_b[pl.ds(plane, 1)] = small[pl.ds(plane, 1)]
    sent_p = scatter(lambda o: small.at[o], small_b, p_send, p_recv, plane, 2 * E, by_plane)
    for i in range(slab):
        begin = i % lines * zonal
        mine = looks[i // lines, pl.ds(ens, 1)][0].astype(F32)
        outlook[:, i, :] = mine[:, begin : begin + zonal]
    look_o[0] = outlook[0:quantities].astype(BF16)
    arrive(rec_b, b_send, b_recv, ens, E, by_ens)
    total = rec_b[0]
    for e in range(1, E):
        total = total + rec_b[e]
    part_c[...] = total
    rec_c[pl.ds(z, 1)] = part_c[pl.ds(z, 1)]
    sent_c = scatter(lambda o: part_c.at[o], rec_c, c_send, c_recv, z, Z, by_z)
    arrive(small_b, p_send, p_recv, plane, 2 * E, by_plane)
    total = small_b[0]
    for o in range(1, 2 * E):
        total = total + small_b[o]
    small_pc[...] = total
    small_c[pl.ds(z, 1)] = total[None]
    sent_q = scatter(lambda o: small_pc, small_c, q_send, q_recv, z, Z, by_z)

    for i in range(slab):
        spread_o[0, :, i, :] = truths[0:quantities, i * zonal : (i + 1) * zonal]
    for copy in own + forwards + shares + [halves] + sent_b:
        copy.wait_send()

    @pl.when(lat < L - 1)
    def _():
        south.wait_send()

    @pl.when(lat > 0)
    def _():
        north.wait_send()

    arrive(rec_c, c_send, c_recv, z, Z, by_z)
    total = rec_c[0]
    for o in range(1, Z):
        total = total + rec_c[o]
    rec_d[pl.ds(ens, 1)] = total[None]
    sent_d = scatter(lambda e: rec_d.at[ens], rec_d, d_send, d_recv, ens, E, by_ens)
    arrive(small_c, q_send, q_recv, z, Z, by_z)
    total = small_c[0]
    for o in range(1, Z):
        total = total + small_c[o]
    small_d[pl.ds(plane, 1)] = total[None]
    sent_r = scatter(lambda o: small_d.at[plane], small_d, r_send, r_recv, plane, 2 * E, by_plane)
    arrive(rec_d, d_send, d_recv, ens, E, by_ens)
    for e in range(E):
        down_o[e * piece : (e + 1) * piece, :] = rec_d[e, 0:piece]
        up_o[e * piece : (e + 1) * piece, :] = rec_d[e, piece : 2 * piece]
    for copy in sent_c + sent_p + sent_d + sent_q:
        copy.wait_send()
    arrive(small_d, r_send, r_recv, plane, 2 * E, by_plane)
    final = jnp.concatenate([small_d[o] for o in range(2 * E)], axis=0)
    out_o[...] = final[:quantities]
    taps_o[...] = final[GRAD_ROW:tail]
    gain_o[...] = final[tail : tail + 1]
    crps_o[...] = final[tail + 1 : tail + 2, 0:1]

    for copy in sent_r:
        copy.wait_send()


def finish_kernel(*refs):
    count = (len(refs) - 1) // 2
    copies = [
        pltpu.make_async_copy(refs[n], refs[count + n], refs[-1].at[n]) for n in range(count)
    ]
    for copy in copies:
        copy.start()
    for copy in copies:
        copy.wait()


def on_device(
    features, random_perturbation, observed_truth, stencil_taps,
    affine_factor, widen_matrix, shrink_matrix, readout_matrix,
):
    E, L = lax.axis_size("ens"), lax.axis_size("lat")
    Z = L // 2
    _, slab, zonal, channels = random_perturbation.shape
    quantities = readout_matrix.shape[0]
    unit = widen_matrix.shape[0]
    hidden = unit * L
    piece = unit // E
    points = slab * zonal
    parts = slab
    rows = -(-quantities // 16) * 16
    chunk = SMALL_ROWS // (2 * E)
    vmem = pl.BlockSpec(memory_space=pltpu.VMEM)
    dma = pltpu.SemaphoreType.DMA
    out = jax.ShapeDtypeStruct
    hbm = pl.BlockSpec(memory_space=pltpu.HBM)
    grid = (1, quantities, slab, zonal)
    shapes = [
        out((1, 1), F32),
        out((SIDE * SIDE, channels), F32),
        out((1, channels), F32),
        out((unit, channels), F32),
        out((unit, channels), F32),
        out((quantities, channels), F32),
        out(grid, BF16),
        out(grid, F32),
    ]
    results = pl.pallas_call(
        functools.partial(kernel, (E, L)),
        out_shape=shapes,
        in_specs=[hbm] * 8,
        out_specs=[vmem] * 8,
        scratch_shapes=[
            pltpu.VMEM((slab, zonal, channels), BF16),
            pltpu.VMEM((1, slab, zonal, channels), BF16),
            pltpu.VMEM((quantities, slab, zonal), F32),
            pltpu.VMEM((SIDE * SIDE, channels), F32),
            pltpu.VMEM((1, channels), F32),
            pltpu.VMEM((quantities, channels), BF16),
            pltpu.VMEM((slab + 2 * HALF, zonal, channels), BF16),
            pltpu.VMEM((slab + 2 * HALF, zonal + 2 * PAD, channels), F32),
            pltpu.VMEM((SIDE * SIDE, 8, channels), F32),
            pltpu.VMEM((slab, zonal, channels), F32),
            pltpu.VMEM((slab, zonal, channels), F32),
            pltpu.VMEM((slab, zonal, channels), F32),
            pltpu.VMEM((points, channels), BF16),
            pltpu.VMEM((points, hidden), F32),
            pltpu.VMEM((points, hidden), F32),
            pltpu.VMEM((points, hidden), BF16),
            pltpu.VMEM((rows, channels), BF16),
            pltpu.VMEM((parts, E, rows, points // parts), BF16),
            pltpu.VMEM((L, 2, unit, channels), BF16),
            pltpu.VMEM((points, channels), BF16),
            pltpu.VMEM((rows, points), BF16),
            pltpu.VMEM((points, channels), BF16),
            pltpu.VMEM((points, hidden), BF16),
            pltpu.VMEM((rows, slab, zonal), F32),
            pltpu.VMEM((rows, points), F32),
            pltpu.VMEM((SIDE * SIDE, channels), F32),
            pltpu.VMEM((2, E, Z, 2 * piece, channels), F32),
            pltpu.VMEM((E, Z, 2 * piece, channels), F32),
            pltpu.VMEM((E, Z, 2 * piece, channels), F32),
            pltpu.VMEM((E, Z, 2 * piece, channels), F32),
            pltpu.VMEM((Z, 2 * piece, channels), F32),
            pltpu.VMEM((Z, 2 * piece, channels), F32),
            pltpu.VMEM((E, 2 * piece, channels), F32),
            pltpu.VMEM((2 * E, chunk, channels), F32),
            pltpu.VMEM((2 * E, chunk, channels), F32),
            pltpu.VMEM((chunk, channels), F32),
            pltpu.VMEM((Z, chunk, channels), F32),
            pltpu.VMEM((2 * E, chunk, channels), F32),
            dma((8,)), dma((2,)), dma((2,)),
            dma((Z,)), dma((Z,)), dma((L,)),
            dma((slab, E)), dma((slab, E)),
            dma((1,)), dma((1,)),
            dma((E,)), dma((E,)),
            dma((Z,)), dma((Z,)),
            dma((E,)), dma((E,)),
            dma((2 * E,)), dma((2 * E,)),
            dma((Z,)), dma((Z,)),
            dma((2 * E,)), dma((2 * E,)),
        ],
        compiler_params=pltpu.CompilerParams(
            collective_id=0, has_side_effects=True, vmem_limit_bytes=40 * 1024 * 1024
        ),
        cost_estimate=pl.CostEstimate(
            flops=12 * points * channels * hidden, bytes_accessed=2_000_000, transcendentals=0
        ),
    )(
        *[
            pltpu.with_memory_space_constraint(value, pltpu.HBM)
            for value in (
                features, random_perturbation, observed_truth, stencil_taps,
                affine_factor.reshape(1, channels), widen_matrix, shrink_matrix, readout_matrix,
            )
        ]
    )
    crps, taps, gain, up, down, head, look, spread = pl.pallas_call(
        finish_kernel,
        out_shape=shapes,
        in_specs=[vmem] * 8,
        out_specs=[hbm] * 8,
        scratch_shapes=[dma((8,))],
        compiler_params=pltpu.CompilerParams(vmem_limit_bytes=8 * 1024 * 1024),
    )(*results)
    return (
        crps.reshape(()), taps, gain.reshape(channels), up, down, head, look, spread,
    )


def solution(mesh):
    in_specs = (
        P("lat", None, None),
        P("ens", "lat", None, None),
        P(None, "lat", None),
        P(),
        P(),
        P("lat", None),
        P("lat", None),
        P(),
    )
    out_specs = (
        P(),
        P(),
        P(),
        P("lat", None),
        P("lat", None),
        P(),
        P("ens", None, "lat", None),
        P("ens", None, "lat", None),
    )
    return jax.shard_map(
        on_device, mesh=mesh, in_specs=in_specs, out_specs=out_specs, check_vma=False
    )
```

```python
import functools
import math

import jax
import jax.numpy as jnp
from jax import lax
from jax.experimental import pallas as pl
from jax.experimental.pallas import tpu as pltpu
from jax.sharding import PartitionSpec as P

SIDE = 7
HALF = SIDE // 2
SQRT_TWO_PI = 0.7978845608028654
CUBIC = 0.044715
EPSILON = 1e-06
SMOOTHING = 0.01
PAD = 8
GRAD_ROW = 72
SMALL_ROWS = 128
F32 = jnp.float32
BF16 = jnp.bfloat16


def dot(a, b, dims):
    return lax.dot_general(a, b, (dims, ((), ())), preferred_element_type=F32)


def kernel(
    sizes,
    feat_h, noise_h, obs_h, taps_h, gain_h, widen_h, shrink_h, readout_h,
    crps_o, taps_o, gain_o, up_o, down_o, out_o, look_o, spread_o,
    feat, noise, obs, taps, gain, readout,
    ext, wide, tapb, depth, scaled_s, inv_s, normed, upper, inner, gated, ro, looks, wbuf,
    resid, flows, back, gated_back, outlook, truths, tap_grad,
    grads, rec_a, part_b, rec_b, part_c, rec_c, rec_d,
    small, small_b, small_pc, small_c, small_d,
    in_sem, halo_send, halo_recv, w_send, w_fwd, w_recv, e_send, e_recv,
    a_send, a_recv, b_send, b_recv, c_send, c_recv, d_send, d_recv,
    p_send, p_recv, q_send, q_recv, r_send, r_recv,
):
    E, L = sizes
    Z = L // 2
    slab, zonal, channels = feat.shape
    quantities = obs.shape[0]
    rows = ro.shape[0]
    points = slab * zonal
    hidden = L * wbuf.shape[2]
    piece = wbuf.shape[2] // E
    ens = lax.axis_index("ens")
    lat = lax.axis_index("lat")
    z = lat // 2
    core = lat % 2
    sibling = z * 2 + (1 - core)

    def at(e, l):
        return {"ens": e, "lat": l}

    def remote(src, dst, send, recv, where):
        return pltpu.make_async_remote_copy(
            src_ref=src, dst_ref=dst, send_sem=send, recv_sem=recv,
            device_id=where, device_id_type=pl.DeviceIdType.MESH,
        )

    barrier = pltpu.get_barrier_semaphore()
    for k in range(1, L):
        pl.semaphore_signal(barrier, inc=1, device_id=at(ens, (lat + k) % L),
                            device_id_type=pl.DeviceIdType.MESH)
    for k in range(1, E):
        for l in (lat, sibling):
            pl.semaphore_signal(barrier, inc=1, device_id=at((ens + k) % E, l),
                                device_id_type=pl.DeviceIdType.MESH)

    loads = [
        pltpu.make_async_copy(src, dst, in_sem.at[n])
        for n, (src, dst) in enumerate([
            (feat_h, feat), (noise_h, noise), (widen_h, wbuf.at[lat, 0]),
            (shrink_h, wbuf.at[lat, 1]), (taps_h, taps), (readout_h, readout),
            (gain_h, gain), (obs_h, obs),
        ])
    ]
    for copy in loads:
        copy.start()

    def widen_rows(start, count):
        block = ext[start : start + count].astype(F32)
        wide[start : start + count, PAD : PAD + zonal, :] = block
        wide[start : start + count, 0:PAD, :] = block[:, zonal - PAD :, :]
        wide[start : start + count, PAD + zonal :, :] = block[:, :PAD, :]

    pl.semaphore_wait(barrier, L - 1 + 2 * (E - 1))
    loads[2].wait()
    loads[3].wait()
    own = [
        remote(wbuf.at[lat], wbuf.at[lat], w_send.at[k], w_recv.at[lat],
               at(ens, ((z + k) % Z) * 2 + core))
        for k in range(1, Z)
    ]
    for copy in own:
        copy.start()
    forwards = [remote(wbuf.at[lat], wbuf.at[lat], w_fwd.at[0], w_recv.at[lat], at(ens, sibling))]
    forwards[0].start()

    loads[0].wait()
    loads[1].wait()
    field = (feat[...].astype(F32) + noise[0].astype(F32)).astype(BF16)
    ext[HALF : HALF + slab] = field

    south = remote(ext.at[pl.ds(slab, HALF)], ext.at[pl.ds(0, HALF)],
                   halo_send.at[0], halo_recv.at[0], at(ens, jnp.minimum(lat + 1, L - 1)))
    north = remote(ext.at[pl.ds(HALF, HALF)], ext.at[pl.ds(HALF + slab, HALF)],
                   halo_send.at[1], halo_recv.at[1], at(ens, jnp.maximum(lat - 1, 0)))

    @pl.when(lat < L - 1)
    def _():
        south.start()

    @pl.when(lat > 0)
    def _():
        north.start()

    widen_rows(HALF, slab)
    for copy in loads[4:]:
        copy.wait()
    for t in range(SIDE * SIDE):
        tapb[t] = jnp.broadcast_to(taps[t : t + 1, :], (8, channels))
    ro[...] = jnp.zeros_like(ro)
    ro[0:quantities, :] = readout[...]

    step = 32

    def convolve(ext_rows, fresh):
        def body(t, carry):
            base = pl.multiple_of(t * step, step)
            sums = []
            for i in range(slab):
                if fresh:
                    sums.append(jnp.zeros((step // 8, 8, channels), F32))
                else:
                    sums.append(depth[i, pl.ds(base, step), :].reshape(step // 8, 8, channels))
            for b in range(SIDE):
                for r in ext_rows:
                    x = wide[r, pl.ds(base + PAD - HALF + b, step), :].reshape(
                        step // 8, 8, channels)
                    for i in range(slab):
                        a = r - i
                        if 0 <= a < SIDE:
                            sums[i] = sums[i] + tapb[a * SIDE + b] * x
            for i in range(slab):
                depth[i, pl.ds(base, step), :] = sums[i].reshape(step, channels)
            return carry

        lax.fori_loop(0, zonal // step, body, 0)

    convolve(range(HALF, HALF + slab), True)

    latitudes = slab * L
    row = lax.broadcasted_iota(jnp.int32, (slab, zonal), 0) + lat * slab
    area = jnp.cos(math.pi * ((row.astype(F32) + 0.5) / latitudes - 0.5))
    weights = area * (1.0 / (latitudes * zonal))
    truths[...] = jnp.zeros_like(truths)
    for i in range(slab):
        truths[0:quantities, i * zonal : (i + 1) * zonal] = obs[:, i, :]

    for k in range(1, Z):
        other = ((z + k) % Z) * 2 + core
        remote(wbuf.at[other], wbuf.at[other], w_send.at[k], w_recv.at[other],
               at(ens, other)).wait_recv()
        copy = remote(wbuf.at[other], wbuf.at[other], w_fwd.at[k], w_recv.at[other],
                      at(ens, sibling))
        copy.start()
        forwards.append(copy)

    @pl.when(lat > 0)
    def _():
        south.wait_recv()
        widen_rows(0, HALF)

    @pl.when(lat == 0)
    def _():
        wide[0:HALF] = jnp.zeros((HALF, zonal + 2 * PAD, channels), F32)

    @pl.when(lat < L - 1)
    def _():
        north.wait_recv()
        widen_rows(HALF + slab, HALF)

    @pl.when(lat == L - 1)
    def _():
        wide[HALF + slab :] = jnp.zeros((HALF, zonal + 2 * PAD, channels), F32)

    convolve([*range(HALF), *range(HALF + slab, 2 * HALF + slab)], False)

    for i in range(slab):
        d = depth[i]
        centred = d - jnp.mean(d, axis=-1, keepdims=True)
        inverse = lax.rsqrt(jnp.mean(centred * centred, axis=-1, keepdims=True) + EPSILON)
        scaled = centred * inverse
        scaled_s[i] = scaled
        inv_s[i] = jnp.broadcast_to(inverse, (zonal, channels))
        normed[i * zonal : (i + 1) * zonal, :] = (gain[...] * scaled).astype(BF16)

    for k in range(Z):
        other = ((z + k) % Z) * 2 + (1 - core)
        remote(wbuf.at[other], wbuf.at[other], w_fwd.at[k], w_recv.at[other],
               at(ens, sibling)).wait_recv()

    up = wbuf[:, 0].reshape(hidden, channels)
    down = wbuf[:, 1].reshape(hidden, channels)
    sub = 32
    shares = []
    parts = slab
    span = points // parts
    lines = slab // parts
    def activate(i):
        for t in range(i * span, (i + 1) * span, sub):
            u = upper[t : t + sub, :]
            th = jnp.tanh(SQRT_TWO_PI * (u + CUBIC * u * u * u))
            inner[t : t + sub, :] = th
            gated[t : t + sub, :] = (0.5 * u * (1.0 + th)).astype(BF16)

    upper[...] = dot(normed[...], up, ((1,), (1,)))
    activate(0)
    for i in range(parts):
        begin, end = i * span, (i + 1) * span
        if i + 1 < parts:
            activate(i + 1)
        mixed = dot(gated[begin:end, :], down, ((1,), (0,)))
        field = ext[HALF + i * lines : HALF + (i + 1) * lines].reshape(span, channels)
        residual = (field.astype(F32) + mixed).astype(BF16)
        resid[begin:end, :] = residual
        mine = dot(ro[...], residual, ((1,), (1,))).astype(BF16)
        looks[i, pl.ds(ens, 1)] = mine[None]
        for k in range(1, E):
            copy = remote(looks.at[i, ens], looks.at[i, ens], e_send.at[i, k], e_recv.at[i, ens],
                          at((ens + k) % E, lat))
            copy.start()
            shares.append(copy)


    for t in range(0, points, sub):
        u = upper[t : t + sub, :]
        th = inner[t : t + sub, :]
        inner[t : t + sub, :] = 0.5 * (1.0 + th) + 0.5 * u * (1.0 - th * th) * SQRT_TWO_PI * (
            1.0 + 3.0 * CUBIC * u * u
        )

    members = E
    pair_norm = 1.0 / (members * (members - 1))
    def descend(i):
        begin, end = i * span, (i + 1) * span
        back_residual = dot(flows[:, begin:end], ro[...], ((0,), (0,))).astype(BF16)
        back[begin:end, :] = back_residual
        upper[begin:end, :] = dot(back_residual, down, ((1,), (1,)))
        for t in range(begin, end, sub):
            gated_back[t : t + sub, :] = (
                upper[t : t + sub, :] * inner[t : t + sub, :]).astype(BF16)

    loss = jnp.zeros((1, span), F32)
    for i in range(parts):
        begin, end = i * span, (i + 1) * span
        weight = jnp.concatenate(
            [weights[i * lines + n : i * lines + n + 1] for n in range(lines)], axis=1)
        mine = looks[i, pl.ds(ens, 1)][0].astype(F32)
        miss = mine - truths[:, begin:end]
        square = miss * miss + SMOOTHING
        root = lax.rsqrt(square)
        miss_size = square * root
        miss_slope = miss * root
        spread = jnp.full((rows, span), math.sqrt(SMOOTHING), F32)
        ranks = jnp.zeros((rows, span), F32)
        for k in range(1, E):
            other = (ens + k) % E
            remote(looks.at[i, other], looks.at[i, other], e_send.at[i, k], e_recv.at[i, other],
                   at(other, lat)).wait_recv()
            gap = mine - looks[i, pl.ds(other, 1)][0].astype(F32)
            square = gap * gap + SMOOTHING
            root = lax.rsqrt(square)
            spread = spread + square * root
            ranks = ranks + gap * root
        truths[:, begin:end] = spread * (1.0 / (members - 1))
        part = weight * (miss_size / members - 0.5 * pair_norm * spread)
        loss = loss + jnp.sum(part[:quantities], axis=0, keepdims=True)
        flow = (weight * (miss_slope / members - pair_norm * ranks)).astype(BF16)
        flows[:, begin:end] = flow
        if i > 0:
            descend(i - 1)
    descend(parts - 1)
    loss = jnp.sum(loss, axis=1, keepdims=True)

    def stash(slot, value):
        for l in range(L):
            for e in range(E):
                begin = (l * E + e) * piece
                grads[l % 2, e, l // 2, slot * piece : (slot + 1) * piece] = (
                    value[begin : begin + piece])

    def scatter(src, dst, send, recv, me, count, place):
        copies = [
            remote(src((me + k) % count), dst.at[me], send.at[k], recv.at[me],
                   place((me + k) % count))
            for k in range(1, count)
        ]
        for copy in copies:
            copy.start()
        return copies

    def arrive(dst, send, recv, me, count, place):
        for k in range(1, count):
            other = (me + k) % count
            remote(dst.at[other], dst.at[other], send.at[k], recv.at[other],
                   place(other)).wait_recv()

    def by_ens(e):
        return at(e, lat)

    def by_z(other):
        return at(ens, other * 2 + core)

    stash(0, dot(gated[...], back[...], ((0,), (0,))))
    stash(1, dot(gated_back[...], normed[...], ((0,), (0,))))
    halves = remote(grads.at[1 - core], rec_a, a_send.at[0], a_recv.at[0], at(ens, sibling))
    halves.start()

    out_grad = dot(flows[...], resid[...], ((1,), (0,)))
    chunk = SMALL_ROWS // (2 * E)

    def put(row, value):
        done = 0
        count = value.shape[0]
        while done < count:
            block, offset = divmod(row + done, chunk)
            take = min(count - done, chunk - offset)
            small[block, offset : offset + take, :] = value[done : done + take]
            done += take

    put(0, out_grad[:GRAD_ROW])

    upper[:, 0:channels] = dot(gated_back[...], up, ((1,), (0,)))
    gain_sum = jnp.zeros((1, channels), F32)
    for i in range(slab):
        if i == slab // 2:
            halves.wait_recv()
            part_b[...] = grads[pl.ds(core, 1)][0] + rec_a[...]
            rec_b[pl.ds(ens, 1)] = part_b[pl.ds(ens, 1)]
            sent_b = scatter(lambda e: part_b.at[e], rec_b, b_send, b_recv, ens, E, by_ens)
        back_norm = upper[i * zonal : (i + 1) * zonal, 0:channels]
        scaled = scaled_s[i]
        gain_sum = gain_sum + jnp.sum(back_norm * scaled, axis=0, keepdims=True)
        g = back_norm * gain[...]
        depth[i] = inv_s[i] * (
            g
            - jnp.mean(g, axis=-1, keepdims=True)
            - scaled * jnp.mean(g * scaled, axis=-1, keepdims=True)
        )
    lane = 32

    def tap_columns(b, carry):
        sums = [jnp.zeros((8, channels), F32) for _ in range(SIDE)]
        for base in range(0, zonal, lane):
            g = [depth[i, base : base + lane, :] for i in range(slab)]
            wides = [jnp.zeros((lane, channels), F32)] * SIDE
            for r in range(2 * HALF + slab):
                x = wide[r, pl.ds(base + PAD - HALF + b, lane), :]
                for i in range(slab):
                    a = r - i
                    if 0 <= a < SIDE:
                        wides[a] = wides[a] + g[i] * x
            for a in range(SIDE):
                sums[a] = sums[a] + jnp.sum(wides[a].reshape(lane // 8, 8, channels), axis=0)
        for a in range(SIDE):
            tap_grad[pl.ds(a * SIDE + b, 1), :] = jnp.sum(sums[a], axis=0, keepdims=True)
        return carry

    lax.fori_loop(0, SIDE, tap_columns, 0)
    put(GRAD_ROW, tap_grad[...])
    tail = GRAD_ROW + SIDE * SIDE
    put(tail, gain_sum)
    put(tail + 1, jnp.broadcast_to(loss, (1, channels)))
    put(tail + 2, jnp.zeros((SMALL_ROWS - tail - 2, channels), F32))

    plane = ens * 2 + core

    def by_plane(o):
        return at(o // 2, z * 2 + o % 2)

    small_b[pl.ds(plane, 1)] = small[pl.ds(plane, 1)]
    sent_p = scatter(lambda o: small.at[o], small_b, p_send, p_recv, plane, 2 * E, by_plane)
    for i in range(slab):
        begin = i % lines * zonal
        mine = looks[i // lines, pl.ds(ens, 1)][0].astype(F32)
        outlook[:, i, :] = mine[:, begin : begin + zonal]
    look_o[0] = outlook[0:quantities].astype(BF16)
    arrive(rec_b, b_send, b_recv, ens, E, by_ens)
    total = rec_b[0]
    for e in range(1, E):
        total = total + rec_b[e]
    part_c[...] = total
    rec_c[pl.ds(z, 1)] = part_c[pl.ds(z, 1)]
    sent_c = scatter(lambda o: part_c.at[o], rec_c, c_send, c_recv, z, Z, by_z)
    arrive(small_b, p_send, p_recv, plane, 2 * E, by_plane)
    total = small_b[0]
    for o in range(1, 2 * E):
        total = total + small_b[o]
    small_pc[...] = total
    small_c[pl.ds(z, 1)] = total[None]
    sent_q = scatter(lambda o: small_pc, small_c, q_send, q_recv, z, Z, by_z)

    for i in range(slab):
        spread_o[0, :, i, :] = truths[0:quantities, i * zonal : (i + 1) * zonal]
    for copy in own + forwards + shares + [halves] + sent_b:
        copy.wait_send()

    @pl.when(lat < L - 1)
    def _():
        south.wait_send()

    @pl.when(lat > 0)
    def _():
        north.wait_send()

    arrive(rec_c, c_send, c_recv, z, Z, by_z)
    total = rec_c[0]
    for o in range(1, Z):
        total = total + rec_c[o]
    rec_d[pl.ds(ens, 1)] = total[None]
    sent_d = scatter(lambda e: rec_d.at[ens], rec_d, d_send, d_recv, ens, E, by_ens)
    arrive(small_c, q_send, q_recv, z, Z, by_z)
    total = small_c[0]
    for o in range(1, Z):
        total = total + small_c[o]
    small_d[pl.ds(plane, 1)] = total[None]
    sent_r = scatter(lambda o: small_d.at[plane], small_d, r_send, r_recv, plane, 2 * E, by_plane)
    arrive(rec_d, d_send, d_recv, ens, E, by_ens)
    for e in range(E):
        down_o[e * piece : (e + 1) * piece, :] = rec_d[e, 0:piece]
        up_o[e * piece : (e + 1) * piece, :] = rec_d[e, piece : 2 * piece]
    for copy in sent_c + sent_p + sent_d + sent_q:
        copy.wait_send()
    arrive(small_d, r_send, r_recv, plane, 2 * E, by_plane)
    final = jnp.concatenate([small_d[o] for o in range(2 * E)], axis=0)
    out_o[...] = final[:quantities]
    taps_o[...] = final[GRAD_ROW:tail]
    gain_o[...] = final[tail : tail + 1]
    crps_o[...] = final[tail + 1 : tail + 2, 0:1]

    for copy in sent_r:
        copy.wait_send()


def finish_kernel(*refs):
    count = (len(refs) - 1) // 2
    copies = [
        pltpu.make_async_copy(refs[n], refs[count + n], refs[-1].at[n]) for n in range(count)
    ]
    for copy in copies:
        copy.start()
    for copy in copies:
        copy.wait()


def on_device(
    features, random_perturbation, observed_truth, stencil_taps,
    affine_factor, widen_matrix, shrink_matrix, readout_matrix,
):
    E, L = lax.axis_size("ens"), lax.axis_size("lat")
    Z = L // 2
    _, slab, zonal, channels = random_perturbation.shape
    quantities = readout_matrix.shape[0]
    unit = widen_matrix.shape[0]
    hidden = unit * L
    piece = unit // E
    points = slab * zonal
    parts = slab
    rows = -(-quantities // 16) * 16
    chunk = SMALL_ROWS // (2 * E)
    vmem = pl.BlockSpec(memory_space=pltpu.VMEM)
    dma = pltpu.SemaphoreType.DMA
    out = jax.ShapeDtypeStruct
    hbm = pl.BlockSpec(memory_space=pltpu.HBM)
    grid = (1, quantities, slab, zonal)
    shapes = [
        out((1, 1), F32),
        out((SIDE * SIDE, channels), F32),
        out((1, channels), F32),
        out((unit, channels), F32),
        out((unit, channels), F32),
        out((quantities, channels), F32),
        out(grid, BF16),
        out(grid, F32),
    ]
    results = pl.pallas_call(
        functools.partial(kernel, (E, L)),
        out_shape=shapes,
        in_specs=[hbm] * 8,
        out_specs=[vmem] * 8,
        scratch_shapes=[
            pltpu.VMEM((slab, zonal, channels), BF16),
            pltpu.VMEM((1, slab, zonal, channels), BF16),
            pltpu.VMEM((quantities, slab, zonal), F32),
            pltpu.VMEM((SIDE * SIDE, channels), F32),
            pltpu.VMEM((1, channels), F32),
            pltpu.VMEM((quantities, channels), BF16),
            pltpu.VMEM((slab + 2 * HALF, zonal, channels), BF16),
            pltpu.VMEM((slab + 2 * HALF, zonal + 2 * PAD, channels), F32),
            pltpu.VMEM((SIDE * SIDE, 8, channels), F32),
            pltpu.VMEM((slab, zonal, channels), F32),
            pltpu.VMEM((slab, zonal, channels), F32),
            pltpu.VMEM((slab, zonal, channels), F32),
            pltpu.VMEM((points, channels), BF16),
            pltpu.VMEM((points, hidden), F32),
            pltpu.VMEM((points, hidden), F32),
            pltpu.VMEM((points, hidden), BF16),
            pltpu.VMEM((rows, channels), BF16),
            pltpu.VMEM((parts, E, rows, points // parts), BF16),
            pltpu.VMEM((L, 2, unit, channels), BF16),
            pltpu.VMEM((points, channels), BF16),
            pltpu.VMEM((rows, points), BF16),
            pltpu.VMEM((points, channels), BF16),
            pltpu.VMEM((points, hidden), BF16),
            pltpu.VMEM((rows, slab, zonal), F32),
            pltpu.VMEM((rows, points), F32),
            pltpu.VMEM((SIDE * SIDE, channels), F32),
            pltpu.VMEM((2, E, Z, 2 * piece, channels), F32),
            pltpu.VMEM((E, Z, 2 * piece, channels), F32),
            pltpu.VMEM((E, Z, 2 * piece, channels), F32),
            pltpu.VMEM((E, Z, 2 * piece, channels), F32),
            pltpu.VMEM((Z, 2 * piece, channels), F32),
            pltpu.VMEM((Z, 2 * piece, channels), F32),
            pltpu.VMEM((E, 2 * piece, channels), F32),
            pltpu.VMEM((2 * E, chunk, channels), F32),
            pltpu.VMEM((2 * E, chunk, channels), F32),
            pltpu.VMEM((chunk, channels), F32),
            pltpu.VMEM((Z, chunk, channels), F32),
            pltpu.VMEM((2 * E, chunk, channels), F32),
            dma((8,)), dma((2,)), dma((2,)),
            dma((Z,)), dma((Z,)), dma((L,)),
            dma((slab, E)), dma((slab, E)),
            dma((1,)), dma((1,)),
            dma((E,)), dma((E,)),
            dma((Z,)), dma((Z,)),
            dma((E,)), dma((E,)),
            dma((2 * E,)), dma((2 * E,)),
            dma((Z,)), dma((Z,)),
            dma((2 * E,)), dma((2 * E,)),
        ],
        compiler_params=pltpu.CompilerParams(
            collective_id=0, has_side_effects=True, vmem_limit_bytes=40 * 1024 * 1024
        ),
        cost_estimate=pl.CostEstimate(
            flops=12 * points * channels * hidden, bytes_accessed=2_000_000, transcendentals=0
        ),
    )(
        *[
            pltpu.with_memory_space_constraint(value, pltpu.HBM)
            for value in (
                features, random_perturbation, observed_truth, stencil_taps,
                affine_factor.reshape(1, channels), widen_matrix, shrink_matrix, readout_matrix,
            )
        ]
    )
    crps, taps, gain, up, down, head, look, spread = pl.pallas_call(
        finish_kernel,
        out_shape=shapes,
        in_specs=[vmem] * 8,
        out_specs=[hbm] * 8,
        scratch_shapes=[dma((8,))],
        compiler_params=pltpu.CompilerParams(vmem_limit_bytes=8 * 1024 * 1024),
    )(*results)
    return (
        crps.reshape(()), taps, gain.reshape(channels), up, down, head, look, spread,
    )


def solution(mesh):
    in_specs = (
        P("lat", None, None),
        P("ens", "lat", None, None),
        P(None, "lat", None),
        P(),
        P(),
        P("lat", None),
        P("lat", None),
        P(),
    )
    out_specs = (
        P(),
        P(),
        P(),
        P("lat", None),
        P("lat", None),
        P(),
        P("ens", None, "lat", None),
        P("ens", None, "lat", None),
    )
    return jax.shard_map(
        on_device, mesh=mesh, in_specs=in_specs, out_specs=out_specs, check_vma=False
    )
```
